32 devices in a mesh: parts: 2 (over y), blk: 4 (over z), sub: 4 (over x, core).
Axes of the slice: x: 2, y: 2, z: 4, core: 2. Of those that a mesh axis runs over, the one named last changes fastest.
Arguments:
- embeddings: bfloat16 [40, 512, 1024], P(('parts', 'blk'), 'sub'), parts along dimension 0, may hold values from -6 to 6
- row_count: int32 [40], P(('parts', 'blk')), parts along dimension 0, may hold values from 128 to 512, as said below
- fetch_list: int32 [8, 5], P('parts'), parts along dimension 0, may hold values from 0 to 19, as said below
- pair_left: int32 [8, 15], P(('parts', 'blk')), parts along dimension 0, may hold values from 0 to 4, as said below
- pair_right: int32 [8, 15], P(('parts', 'blk')), parts along dimension 0, may hold values from 0 to 4, as said below
- pair_count: int32 [8], P(('parts', 'blk')), parts along dimension 0, may hold values from 1 to 15, as said below
Outputs:
- density: float32 [40, 512], P(('parts', 'blk'), 'sub'), parts along dimension 0
The draws below stay inside these ranges and needn't reach their ends.
There are 2 independent parts, one for each index of `parts`. The reference program is written for one: setup_inputs(seed, part) draws one part's arguments, and reference() takes and returns one part's arrays. A program takes and returns all parts, laid end to end along the dimension named above; each array names one. Nothing has to cross between parts.
Inputs may be any that keep to these rules, and one draw needn't show every extreme that they name: `fetch_list`: row s lists 5 blocks, each once, the blocks of one cluster at consecutive positions; every block is in exactly one row. A row holds at most 2 blocks of one index of blk (block b is owned by index b // 5), and 2 of some owner. Entries p < pair_count[s] list every pair of positions i <= j of one cluster of row s of fetch_list once (pair_left i, pair_right j); clusters hold 1 to 5 blocks; later entries are 0. `pair_right`: see pair_left. `pair_count`: some group has 15 pairs. Rows 0 to row_count - 1 of a block are in use; some block has all 512.
All inputs are finite; a program needn't handle non-finite values.
Results may differ from the reference program's by a relative error of at most 0.0003.
Values may be sent and summed in bfloat16 or wider, within the bound.
No kernel may reach another device: no remote copies, remote signals or barrier semaphores. Data moves between devices by JAX's collectives and lax.ppermute only.
A program may use at most 64 MiB of HBM per device.

```python
import jax
import jax.numpy as jnp
from jax import lax

D = 1024
B_DEV = 5
CMAX = 5
BR = 512
NB = 20
CAP = 2
PAIRS = 15
N_BLK = 4


def assignment(key):
    shift_key, order_key = jax.random.split(key)
    shifts = (jax.random.permutation(shift_key, N_BLK * CAP)[:B_DEV] % N_BLK).astype(jnp.int32)
    orders = jax.vmap(lambda sub_key: jax.random.permutation(sub_key, B_DEV))(jax.random.split(order_key, N_BLK)).astype(jnp.int32)
    return (shifts, orders)


def cluster_pairs(key):
    size_key, pick_key = jax.random.split(key)
    block_sizes = jax.random.randint(size_key, (N_BLK, B_DEV), 1, CMAX + 1)
    full_group = jax.random.randint(pick_key, (), 0, N_BLK)
    block_sizes = jnp.where(jnp.arange(N_BLK)[:, None] == full_group, CMAX, block_sizes)
    run_ends = jnp.cumsum(block_sizes, axis=1)
    position = jnp.arange(B_DEV, dtype=jnp.int32)
    cluster = jnp.sum(run_ends[:, None, :] <= position[None, :, None], axis=2)
    pair_mask = (cluster[:, :, None] == cluster[:, None, :]) & (position[:, None] <= position[None, :])[None]
    sort_keys = jnp.where(pair_mask, position[:, None] * B_DEV + position[None, :], B_DEV * B_DEV).reshape(N_BLK, B_DEV * B_DEV)
    ordered = jnp.sort(sort_keys, axis=1)[:, :PAIRS]
    present = ordered < B_DEV * B_DEV
    left_pos = jnp.where(present, ordered // B_DEV, 0).astype(jnp.int32)
    right_pos = jnp.where(present, ordered % B_DEV, 0).astype(jnp.int32)
    pair_total = jnp.sum(pair_mask.reshape(N_BLK, -1), axis=1).astype(jnp.int32)
    return (left_pos, right_pos, pair_total)


def draw_fetch_list(key, part):
    shifts, orders = assignment(key)
    key = jax.random.fold_in(key, 12)
    scorers = jnp.arange(N_BLK, dtype=jnp.int32)[:, None]
    owner_idx = (scorers + shifts[None, :]) % N_BLK
    local_idx = orders[owner_idx, jnp.arange(B_DEV, dtype=jnp.int32)[None, :]]
    listed = owner_idx * B_DEV + local_idx
    shuffles = jax.vmap(lambda sub_key: jax.random.permutation(sub_key, B_DEV))(jax.random.split(key, N_BLK))
    return jnp.take_along_axis(listed, shuffles, axis=1).astype(jnp.int32)


def draw_pair_left(key, part):
    left_pos, right_pos, pair_total = cluster_pairs(key)
    return left_pos


def draw_pair_right(key, part):
    left_pos, right_pos, pair_total = cluster_pairs(key)
    return right_pos


def draw_pair_count(key, part):
    left_pos, right_pos, pair_total = cluster_pairs(key)
    return pair_total


def draw_row_count(key, part):
    key = jax.random.fold_in(key, 31)
    full_key, size_key, pick_key = jax.random.split(key, 3)
    full_rows = jax.random.randint(full_key, (NB,), 0, 2) == 0
    partial_rows = jax.random.randint(size_key, (NB,), BR // 4, BR)
    counts = jnp.where(full_rows, BR, partial_rows)
    counts = counts.at[jax.random.randint(pick_key, (), 0, NB)].set(BR)
    return counts.astype(jnp.int32)


def block_levels(stream_key, shape, shards, least, high):
    def one(dim, shards_of):
        steps = jax.random.uniform(jax.random.fold_in(jax.random.fold_in(stream_key, 6), dim), (shards_of,), jnp.float32, least / len(shards), high / len(shards))
        return jnp.repeat(jnp.exp(steps), shape[dim] // shards_of).reshape((-1,) + (1,) * (len(shape) - dim - 1))

    factor_of = one(*shards[0])
    for cut in shards[1:]:
        factor_of = factor_of * one(*cut)
    return factor_of


def bell_draw(rng, extent, spread, limit, cuts=(), held_as=jnp.bfloat16):
    drawn = spread * jax.random.normal(rng, extent, jnp.float32)
    if cuts:
        drawn = drawn * block_levels(rng, extent, cuts, -0.22, 0.18)
    return jnp.clip(drawn, -limit, limit).astype(held_as)


def setup_inputs(seed: int = 0, part: int = 0) -> dict:
    arg_keys = jax.random.split(jax.random.key(seed), 7)
    part_keys = jax.random.split(jax.random.fold_in(arg_keys[6], part), 7)
    embeddings = bell_draw(part_keys[0], (NB, BR, D), 1.0, 6.0, ((0, 4), (1, 4)))
    row_count = draw_row_count(jax.random.fold_in(jax.random.fold_in(arg_keys[6], part), 71), part)
    fetch_list = draw_fetch_list(jax.random.fold_in(jax.random.fold_in(arg_keys[6], part), 71), part)
    pair_left = draw_pair_left(jax.random.fold_in(jax.random.fold_in(arg_keys[6], part), 71), part)
    pair_right = draw_pair_right(jax.random.fold_in(jax.random.fold_in(arg_keys[6], part), 71), part)
    pair_count = draw_pair_count(jax.random.fold_in(jax.random.fold_in(arg_keys[6], part), 71), part)
    return dict(embeddings=embeddings, row_count=row_count, fetch_list=fetch_list, pair_left=pair_left, pair_right=pair_right, pair_count=pair_count)


kernel_scale = 24.0
norm_eps = 1e-06

def block_inverse(block_rows):
    widened = block_rows.astype(jnp.float32)
    return lax.rsqrt(lax.optimization_barrier(jnp.mean(widened * widened, axis=-1)) + norm_eps)

def reference(embeddings, row_count, fetch_list, pair_left, pair_right, pair_count):
    inverse = lax.map(block_inverse, embeddings)
    left_ids = jnp.take_along_axis(fetch_list, pair_left, axis=1).reshape(-1).astype(jnp.int32)
    right_ids = jnp.take_along_axis(fetch_list, pair_right, axis=1).reshape(-1).astype(jnp.int32)
    pair_live = (jnp.arange(PAIRS, dtype=jnp.int32)[None, :] < pair_count[:, None]).reshape(-1)
    row_ids = jnp.arange(BR, dtype=jnp.int32)

    def add_pair(density_sum, pair_item):
        first, second, pair_on = pair_item
        left_block = lax.dynamic_index_in_dim(embeddings, first, 0, keepdims=False)
        right_block = lax.dynamic_index_in_dim(embeddings, second, 0, keepdims=False)
        left_inv = lax.dynamic_index_in_dim(inverse, first, 0, keepdims=False)
        right_inv = lax.dynamic_index_in_dim(inverse, second, 0, keepdims=False)
        gram_tile = jnp.dot(left_block, right_block.T, preferred_element_type=jnp.float32)
        kernel = jnp.exp(kernel_scale / D * gram_tile * left_inv[:, None] * right_inv[None, :])
        in_use = (row_ids < row_count[first])[:, None] & (row_ids < row_count[second])[None, :]
        in_use = in_use & jnp.logical_not((first == second) & (row_ids[:, None] == row_ids[None, :]))
        kernel = jnp.where(in_use & pair_on, kernel, jnp.float32(0.0))
        row_add = lax.optimization_barrier(jnp.sum(kernel, axis=1))
        col_add = jnp.where(first != second, lax.optimization_barrier(jnp.sum(kernel, axis=0)), jnp.float32(0.0))
        density_sum = density_sum.at[first].add(row_add)
        density_sum = density_sum.at[second].add(col_add)
        return (density_sum, None)
    density_sum, _ = lax.scan(add_pair, jnp.zeros((NB, BR), jnp.float32), (left_ids, right_ids, pair_live))
    return jnp.log1p(density_sum / BR)
```

```python
import functools
import itertools
import math

import jax
import jax.numpy as jnp
from jax import lax
from jax.experimental import pallas as pl
from jax.experimental.pallas import tpu as pltpu
from jax.sharding import PartitionSpec as P

kernel_scale = 24.0
norm_eps = 1e-06
VMEM_LIMIT = 48 * 1024 * 1024
ANY = pl.BlockSpec(memory_space=pl.ANY)
SMEM = pl.BlockSpec(memory_space=pltpu.SMEM)
VMEM = pl.BlockSpec(memory_space=pltpu.VMEM)


def block_patterns(places, capacity, blocks):
    if capacity < 2 or places > 4:
        return []
    cost = lambda counts: sum(c * min(k, places - k) for k, c in enumerate(counts))
    best = {}
    for counts in itertools.product(range(capacity + 1), repeat=places):
        if sum(counts) != blocks:
            continue
        turns = [counts[t:] + counts[:t] for t in range(places)]
        pick = min(turns, key=lambda c: (cost(c), c))
        best[min(turns)] = pick
    return sorted(best.values(), key=cost)


def unary(counts):
    return sum(((1 << c) - 1) << (2 * r) for r, c in enumerate(counts))


def plan_kernel(patterns, places, capacity, me_ref, fetch_ref, count_ref, left_ref, right_ref, pairs_ref,
                emb_ref, plan_ref, info_ref, *rest):
    slots, sems = rest[:-1], rest[-1]
    blocks = count_ref.shape[0]
    me = me_ref[0]
    used = jnp.int32(0)
    for s in range(places):
        seen = jnp.int32(0)
        for p in range(blocks):
            owner = lax.div(fetch_ref[s, p], blocks)
            bit = lax.shift_left(jnp.int32(1), 2 * lax.rem(owner + (places - s), places))
            seen = seen | bit | ((seen & bit) << 1)
        used = used | seen
    choice = jnp.int32(len(patterns))
    shift = jnp.int32(0)
    for m in reversed(range(len(patterns))):
        for t in range(places):
            allowed = unary([patterns[m][(t - r) % places] for r in range(places)])
            fits = (used & ~allowed) == 0
            choice = jnp.where(fits, m, choice)
            shift = jnp.where(fits, t, shift)
    plan_ref[0] = choice
    plan_ref[1] = shift
    mine = lax.rem(me + places - shift, places)
    total = places * capacity
    copies = []
    for k in range(places):
        owner = lax.rem(me + places - k, places)
        target = lax.rem(me + k + places - shift, places)
        place, lid, seen = [jnp.int32(0)] * capacity, [jnp.int32(0)] * capacity, jnp.int32(0)
        send, sent = [jnp.int32(0)] * capacity, jnp.int32(0)
        for p in range(blocks):
            listed = fetch_ref[mine, p]
            hit = lax.div(listed, blocks) == owner
            outward = fetch_ref[target, p]
            goes = lax.div(outward, blocks) == me
            for j in range(capacity):
                place[j] = jnp.where(hit & (seen == j), p, place[j])
                lid[j] = jnp.where(hit & (seen == j), listed - owner * blocks, lid[j])
                send[j] = jnp.where(goes & (sent == j), outward - me * blocks, send[j])
            seen = seen + hit.astype(jnp.int32)
            sent = sent + goes.astype(jnp.int32)
        for j in range(capacity):
            at = k * capacity + j
            copy = pltpu.make_async_copy(emb_ref.at[send[j]], slots[at], sems.at[at])
            copy.start()
            copies.append(copy)
            plan_ref[2 + at] = send[j]
            plan_ref[2 + total + at] = place[j]
            plan_ref[2 + 2 * total + at] = lid[j]
    bits = jnp.int32(0)
    for p in range(left_ref.shape[1]):
        a, b = left_ref[0, p], right_ref[0, p]
        both = lax.shift_left(jnp.int32(1), a * blocks + b) | lax.shift_left(jnp.int32(1), b * blocks + a)
        bits = bits | jnp.where(p < pairs_ref[0], both, 0)
    for b in range(blocks):
        info_ref[b] = count_ref[b]
    info_ref[blocks] = bits
    for copy in copies:
        copy.wait()


def make_plan(patterns, places, capacity, me, embeddings, row_count, fetch_list, left, right, pairs):
    blocks, rows, width = embeddings.shape
    total = places * capacity
    slot = jax.ShapeDtypeStruct((rows, width), embeddings.dtype)
    out = pl.pallas_call(
        functools.partial(plan_kernel, patterns, places, capacity),
        out_shape=[jax.ShapeDtypeStruct((2 + 3 * total,), jnp.int32),
                   jax.ShapeDtypeStruct((blocks + 1,), jnp.int32)] + [slot] * total,
        in_specs=[SMEM] * 6 + [ANY],
        out_specs=[SMEM, SMEM] + [ANY] * total,
        scratch_shapes=[pltpu.SemaphoreType.DMA((total,))],
        name="plan_and_gather",
    )(me, fetch_list, row_count, left, right, pairs, embeddings)
    return out[0], out[1], out[2:]


def meta_kernel(slots, total, plan_ref, sub_ref, *refs):
    infos, meta_ref = refs[:-1], refs[-1]
    blocks = len(slots)
    bits = jnp.int32(0)
    for k, info in enumerate(infos):
        bits = jnp.where(plan_ref[1] == k, info[blocks], bits)
    for b, (k, at) in enumerate(slots):
        meta_ref[b] = infos[k][plan_ref[2 + 2 * total + at]]
        meta_ref[blocks + b] = plan_ref[2 + total + at]
    meta_ref[2 * blocks] = bits
    meta_ref[2 * blocks + 1] = sub_ref[0]


def make_meta(slots, total, plan, sub, infos):
    blocks = len(slots)
    return pl.pallas_call(
        functools.partial(meta_kernel, slots, total),
        out_shape=jax.ShapeDtypeStruct((2 * blocks + 2,), jnp.int32),
        in_specs=[SMEM] * (2 + len(infos)),
        out_specs=SMEM,
        name="block_meta",
    )(plan, sub, *infos)


def score_kernel(blocks, rows, width, pieces, loads, jobs, first, last, outs, meta_ref, *refs):
    refs = list(refs)
    given = [refs.pop(0) for _ in loads]
    acc_in = None if first else refs.pop(0)
    out_refs = [refs.pop(0) for _ in (outs if last else (0,))]
    held, acc, left_scale, gram, sems = refs
    slot_of = {what: i for i, what in enumerate(loads)}
    copies = []
    for i, (b, q) in enumerate(loads):
        copy = pltpu.make_async_copy(given[i], held.at[pl.ds(i * rows, rows)], sems.at[i])
        copy.start()
        copies.append(copy)
    waited = set()

    def ready(b, q):
        i = slot_of[b, q]
        if i not in waited:
            waited.add(i)
            copies[i].wait()
        return i

    eye = lax.broadcasted_iota(jnp.int32, (rows, rows), 0) == lax.broadcasted_iota(jnp.int32, (rows, rows), 1)
    column = lax.broadcasted_iota(jnp.int32, (1, rows), 1)
    row = lax.broadcasted_iota(jnp.int32, (rows, 1), 0)
    sub = meta_ref[2 * blocks + 1]
    bits = meta_ref[2 * blocks]

    def inverse(i):
        wide = held[i * rows:(i + 1) * rows, :].astype(jnp.float32)
        return lax.rsqrt(jnp.sum(wide * wide, axis=1, keepdims=True) * (1.0 / width) + norm_eps)

    def lanes(col):
        return jnp.sum(jnp.where(eye, col, 0.0), axis=0, keepdims=True)

    lefts = sorted({a for lo, hi, _, _ in jobs for a in range(lo, hi)})
    inv_of = {}
    for a in lefts:
        i = ready(a, 0)
        inv = inverse(i)
        inv_of[i] = inv
        left_scale[a * rows:(a + 1) * rows, :] = jnp.broadcast_to(
            inv * (kernel_scale / width * math.log2(math.e)), (rows, rows))
    if first:
        acc[...] = jnp.zeros_like(acc)
    else:
        acc[...] = acc_in[...]
    for lo, hi, b, qs in jobs:
        at = [ready(b, q) for q in qs]
        inv_row, valid = [], []
        for q, i in zip(qs, at):
            inv_row.append(lanes(inv_of[i] if i in inv_of else inverse(i)))
            start = (sub ^ q) * rows
            valid.append((column + start < meta_ref[b]).astype(jnp.float32))
        inv_row = jnp.concatenate(inv_row, axis=1)
        valid = jnp.concatenate(valid, axis=1)
        right = held[at[0] * rows:(at[0] + len(at)) * rows, :]
        lo_slot = slot_of[lo, 0]
        left = held[lo_slot * rows:(lo_slot + hi - lo) * rows, :]
        gram[:(hi - lo) * rows, :len(qs) * rows] = lax.dot_general(
            left, right, (((1,), (1,)), ((), ())), preferred_element_type=jnp.float32)
        for a in range(lo, hi):
            here = slice(a * rows, (a + 1) * rows)
            from_row = (a - lo) * rows
            weight = ((bits >> (meta_ref[blocks + a] * blocks + meta_ref[blocks + b])) & 1).astype(jnp.float32)
            weighed = valid * weight
            part = acc[here, :]
            scale = left_scale[here, :]
            for n, q in enumerate(qs):
                cols = slice(n * rows, (n + 1) * rows)
                tile = jnp.exp2(gram[from_row:from_row + rows, cols] * scale * inv_row[:, cols]) * weighed[:, cols]
                if a == b and q == 0:
                    tile = jnp.where(eye, 0.0, tile)
                part = part + tile
            acc[here, :] = part
    if not last:
        out_refs[0][...] = acc[...]
        return
    for ref, group in zip(out_refs, outs):
        for n, a in enumerate(group):
            total = jnp.sum(acc[a * rows:(a + 1) * rows, :], axis=1, keepdims=True)
            total = jnp.where(row + sub * rows < meta_ref[a], total, 0.0)
            ref[n:n + 1, :] = jnp.log1p(lanes(total) / (pieces * rows))


def score(blocks, pieces, held, meta, jobs, acc=None, outs=None, name="score"):
    rows, width = held[0, 0].shape
    needed = []
    lefts = sorted({a for lo, hi, _, _ in jobs for a in range(lo, hi)})
    for a in lefts:
        needed.append((a, 0))
    for _, _, b, qs in jobs:
        for q in qs:
            needed.append((b, q))
    loads = list(dict.fromkeys(needed))
    jobs = split_runs(jobs, loads)
    wide = max((hi - lo) for lo, hi, _, _ in jobs) * rows, max(len(qs) for _, _, _, qs in jobs) * rows
    sums = jax.ShapeDtypeStruct((blocks * rows, rows), jnp.float32)
    out_shape = [sums] if outs is None else [jax.ShapeDtypeStruct((len(g), rows), jnp.float32) for g in outs]
    flops = sum(2 * (hi - lo) * len(qs) * rows * rows * width for lo, hi, _, qs in jobs)
    result = pl.pallas_call(
        functools.partial(score_kernel, blocks, rows, width, pieces, loads, jobs, acc is None, outs is not None, outs),
        out_shape=out_shape,
        in_specs=[SMEM] + [ANY] * len(loads) + ([] if acc is None else [VMEM]),
        out_specs=[VMEM] * len(out_shape),
        scratch_shapes=[
            pltpu.VMEM((len(loads) * rows, width), jnp.bfloat16),
            pltpu.VMEM((blocks * rows, rows), jnp.float32),
            pltpu.VMEM((blocks * rows, rows), jnp.float32),
            pltpu.VMEM(wide, jnp.float32),
            pltpu.SemaphoreType.DMA((len(loads),)),
        ],
        compiler_params=pltpu.CompilerParams(vmem_limit_bytes=VMEM_LIMIT),
        cost_estimate=pl.CostEstimate(flops=flops, bytes_accessed=len(loads) * rows * width * 2, transcendentals=0),
        name=name,
    )(meta, *[held[what] for what in loads], *([] if acc is None else [acc]))
    return result[0] if outs is None else result


def split_runs(jobs, loads):
    place = {what: i for i, what in enumerate(loads)}
    done = []
    for lo, hi, b, qs in jobs:
        run = []
        for q in qs:
            if run and place[b, q] != place[b, run[-1]] + 1:
                done.append((lo, hi, b, tuple(run)))
                run = []
            run.append(q)
        done.append((lo, hi, b, tuple(run)))
    return done


def place_kernel(slots, plan_ref, *refs):
    out_ref = refs[-1]
    for ref, (group) in zip(refs[:-1], slots):
        for n, at in enumerate(group):
            out_ref[pl.ds(plan_ref[2 + at], 1), :] = ref[n:n + 1, :]


def place_rows(slots, plan, returned, blocks, rows):
    return pl.pallas_call(
        functools.partial(place_kernel, slots),
        out_shape=jax.ShapeDtypeStruct((blocks, rows), jnp.float32),
        in_specs=[SMEM] + [VMEM] * len(returned),
        out_specs=VMEM,
        name="place_rows",
    )(plan, *returned)


def shift_by(array, k, places):
    return lax.ppermute(array, "blk", [(i, (i + k) % places) for i in range(places)])


def swap_with(array, q, pieces):
    return lax.ppermute(array, "sub", [(i, i ^ q) for i in range(pieces)])


def pattern_path(counts, capacity, pieces, sub, plan, info, slots):
    places = len(counts)
    order = sorted((k for k in range(places) if counts[k]), key=lambda k: (k * (places - k), k))
    taken = [(k, k * capacity + j) for k in order for j in range(counts[k])]
    blocks = len(taken)
    rows = slots[0].shape[0]
    infos = [info if k == 0 else shift_by(info, k, places) for k in range(places)]
    meta = make_meta(taken, places * capacity, plan, sub, infos)
    held = {}
    for b, (k, at) in enumerate(taken):
        held[b, 0] = slots[at] if k == 0 else shift_by(slots[at], k, places)
    for b in range(blocks):
        held[b, 2] = swap_with(held[b, 0], 2, pieces)
        held[b, 1] = swap_with(held[b, 0], 1, pieces)
        held[b, 3] = swap_with(held[b, 2], 1, pieces)
    end = blocks - 1
    both = tuple(range(pieces))
    acc = score(blocks, pieces, held, meta, [(0, end, b, both) for b in range(end)], name="score_early")
    acc = score(blocks, pieces, held, meta,
                [(end, blocks, b, both) for b in range(end)] + [(0, blocks, end, (0, 1))], acc, name="score_middle")
    groups = [[b for b in range(blocks) if taken[b][0] == k] for k in order]
    sums = score(blocks, pieces, held, meta, [(0, blocks, end, (2, 3))], acc, groups, name="score_late")
    returned = [s if k == 0 else shift_by(s, places - k, places) for k, s in zip(order, sums)]
    return place_rows([[taken[b][1] for b in g] for g in groups], plan, returned, blocks, rows)


def general_path(capacity, pieces, embeddings, row_count, fetch_list, left, right, pairs):
    places = lax.axis_size("blk")
    me = lax.axis_index("blk")
    sub = lax.axis_index("sub")
    blocks, rows, width = embeddings.shape
    total = places * capacity
    local_ids = jnp.arange(blocks, dtype=jnp.int32)
    slot_ids = jnp.arange(total, dtype=jnp.int32)
    owned = me * blocks + local_ids
    here = fetch_list[:, :, None] == owned[None, None, :]
    scorer = jnp.sum(jnp.where(here, jnp.arange(places, dtype=jnp.int32)[:, None, None], 0), axis=(0, 1))
    same = scorer[:, None] == scorer[None, :]
    rank = jnp.sum(same & (local_ids[None, :] < local_ids[:, None]), axis=1)
    send_slot = scorer * capacity + rank
    placing = send_slot[:, None] == slot_ids[None, :]
    source = jnp.sum(jnp.where(placing, local_ids[:, None], 0), axis=0)
    out_counts = jnp.where(jnp.any(placing, axis=0), jnp.take(row_count, source), 0)
    exchange = lambda x: lax.all_to_all(x, "blk", split_axis=0, concat_axis=0, tiled=True)
    incoming = exchange(jnp.take(embeddings, source, axis=0))
    in_counts = exchange(out_counts)
    wanted = lax.dynamic_index_in_dim(fetch_list, me, 0, keepdims=False)
    owner, local = wanted // blocks, wanted % blocks
    together = owner[:, None] == owner[None, :]
    recv_rank = jnp.sum(together & (local[None, :] < local[:, None]), axis=1)
    recv_slot = owner * capacity + recv_rank
    counts = jnp.take(in_counts, recv_slot, axis=0)
    live = jnp.arange(left.shape[1], dtype=jnp.int32) < pairs[0]
    one = jnp.int32(1)
    hot = lambda at: jnp.where(live[:, None], (at[:, None] == jnp.arange(blocks * blocks)).astype(jnp.int32), 0)
    listed = jnp.max(hot(left[0] * blocks + right[0]) | hot(right[0] * blocks + left[0]), axis=0)
    bits = jnp.sum(listed * lax.shift_left(one, jnp.arange(blocks * blocks, dtype=jnp.int32)))
    meta = jnp.concatenate([counts, local_ids, bits[None], sub[None].astype(jnp.int32)]).astype(jnp.int32)
    held = {}
    for b in range(blocks):
        held[b, 0] = lax.dynamic_index_in_dim(incoming, recv_slot[b], 0, keepdims=False)
        for q in range(1, pieces):
            held[b, q] = swap_with(held[b, 0], q, pieces)
    jobs = [(0, blocks, b, (q, q + 1)) for b in range(blocks) for q in range(0, pieces, 2)]
    (dense,) = score(blocks, pieces, held, meta, jobs, None, [list(range(blocks))], name="score_all")
    back = (recv_slot[None, :] == slot_ids[:, None]).astype(jnp.float32)
    returned = exchange(jnp.sum(back[:, :, None] * dense[None, :, :], axis=1))
    return jnp.take(returned, send_slot, axis=0)


def body(embeddings, row_count, fetch_list, pair_left, pair_right, pair_count):
    places = lax.axis_size("blk")
    pieces = lax.axis_size("sub")
    blocks = embeddings.shape[0]
    capacity = (blocks + places - 1) // places
    given = (embeddings, row_count, fetch_list, pair_left, pair_right, pair_count)
    general = functools.partial(general_path, capacity, pieces)
    patterns = block_patterns(places, capacity, blocks)
    if not patterns or pieces != 4:
        return general(*given)
    me = lax.axis_index("blk").astype(jnp.int32)[None]
    sub = lax.axis_index("sub").astype(jnp.int32)[None]
    plan, info, slots = make_plan(patterns, places, capacity, me, *given)
    branches = [
        lambda plan, info, slots, given, counts=counts: pattern_path(counts, capacity, pieces, sub, plan, info, slots)
        for counts in patterns
    ] + [lambda plan, info, slots, given: general(*given)]
    return lax.switch(plan[0], branches, plan, info, slots, given)


def solution(mesh):
    in_specs = (
        P(("parts", "blk"), "sub", None),
        P(("parts", "blk")),
        P("parts", None),
        P(("parts", "blk"), None),
        P(("parts", "blk"), None),
        P(("parts", "blk")),
    )
    out_specs = P(("parts", "blk"), "sub")
    return jax.shard_map(body, mesh=mesh, in_specs=in_specs, out_specs=out_specs, check_vma=False)
```

```python
import functools
import itertools
import math

import jax
import jax.numpy as jnp
from jax import lax
from jax.experimental import pallas as pl
from jax.experimental.pallas import tpu as pltpu
from jax.sharding import PartitionSpec as P

kernel_scale = 24.0
norm_eps = 1e-06
VMEM_LIMIT = 48 * 1024 * 1024
ANY = pl.BlockSpec(memory_space=pl.ANY)
SMEM = pl.BlockSpec(memory_space=pltpu.SMEM)
VMEM = pl.BlockSpec(memory_space=pltpu.VMEM)


def block_patterns(places, capacity, blocks):
    if capacity < 2 or places > 4:
        return []
    cost = lambda counts: sum(c * min(k, places - k) for k, c in enumerate(counts))
    best = {}
    for counts in itertools.product(range(capacity + 1), repeat=places):
        if sum(counts) != blocks:
            continue
        turns = [counts[t:] + counts[:t] for t in range(places)]
        pick = min(turns, key=lambda c: (cost(c), c))
        best[min(turns)] = pick
    return sorted(best.values(), key=cost)


def unary(counts):
    return sum(((1 << c) - 1) << (2 * r) for r, c in enumerate(counts))


def plan_kernel(patterns, places, capacity, me_ref, fetch_ref, count_ref, left_ref, right_ref, pairs_ref,
                emb_ref, plan_ref, info_ref, *rest):
    slots, sems = rest[:-1], rest[-1]
    blocks = count_ref.shape[0]
    me = me_ref[0]
    used = jnp.int32(0)
    for s in range(places):
        seen = jnp.int32(0)
        for p in range(blocks):
            owner = lax.div(fetch_ref[s, p], blocks)
            bit = lax.shift_left(jnp.int32(1), 2 * lax.rem(owner + (places - s), places))
            seen = seen | bit | ((seen & bit) << 1)
        used = used | seen
    choice = jnp.int32(len(patterns))
    shift = jnp.int32(0)
    for m in reversed(range(len(patterns))):
        for t in range(places):
            allowed = unary([patterns[m][(t - r) % places] for r in range(places)])
            fits = (used & ~allowed) == 0
            choice = jnp.where(fits, m, choice)
            shift = jnp.where(fits, t, shift)
    plan_ref[0] = choice
    plan_ref[1] = shift
    mine = lax.rem(me + places - shift, places)
    total = places * capacity
    copies = []
    for k in range(places):
        owner = lax.rem(me + places - k, places)
        target = lax.rem(me + k + places - shift, places)
        place, lid, seen = [jnp.int32(0)] * capacity, [jnp.int32(0)] * capacity, jnp.int32(0)
        send, sent = [jnp.int32(0)] * capacity, jnp.int32(0)
        for p in range(blocks):
            listed = fetch_ref[mine, p]
            hit = lax.div(listed, blocks) == owner
            outward = fetch_ref[target, p]
            goes = lax.div(outward, blocks) == me
            for j in range(capacity):
                place[j] = jnp.where(hit & (seen == j), p, place[j])
                lid[j] = jnp.where(hit & (seen == j), listed - owner * blocks, lid[j])
                send[j] = jnp.where(goes & (sent == j), outward - me * blocks, send[j])
            seen = seen + hit.astype(jnp.int32)
            sent = sent + goes.astype(jnp.int32)
        for j in range(capacity):
            at = k * capacity + j
            copy = pltpu.make_async_copy(emb_ref.at[send[j]], slots[at], sems.at[at])
            pl.when(sent > j)(copy.start)
            copies.append((sent > j, copy))
            plan_ref[2 + at] = send[j]
            plan_ref[2 + total + at] = place[j]
            plan_ref[2 + 2 * total + at] = lid[j]
    bits = jnp.int32(0)
    for p in range(left_ref.shape[1]):
        a, b = left_ref[0, p], right_ref[0, p]
        both = lax.shift_left(jnp.int32(1), a * blocks + b) | lax.shift_left(jnp.int32(1), b * blocks + a)
        bits = bits | jnp.where(p < pairs_ref[0], both, 0)
    for b in range(blocks):
        info_ref[b] = count_ref[b]
    info_ref[blocks] = bits
    for filled, copy in copies:
        pl.when(filled)(copy.wait)


def make_plan(patterns, places, capacity, me, embeddings, row_count, fetch_list, left, right, pairs):
    blocks, rows, width = embeddings.shape
    total = places * capacity
    slot = jax.ShapeDtypeStruct((rows, width), embeddings.dtype)
    out = pl.pallas_call(
        functools.partial(plan_kernel, patterns, places, capacity),
        out_shape=[jax.ShapeDtypeStruct((2 + 3 * total,), jnp.int32),
                   jax.ShapeDtypeStruct((blocks + 1,), jnp.int32)] + [slot] * total,
        in_specs=[SMEM] * 6 + [ANY],
        out_specs=[SMEM, SMEM] + [VMEM] * total,
        scratch_shapes=[pltpu.SemaphoreType.DMA((total,))],
        name="plan_and_gather",
    )(me, fetch_list, row_count, left, right, pairs, embeddings)
    return out[0], out[1], out[2:]


def meta_kernel(slots, total, plan_ref, sub_ref, *refs):
    infos, meta_ref = refs[:-1], refs[-1]
    blocks = len(slots)
    bits = jnp.int32(0)
    for k, info in enumerate(infos):
        bits = jnp.where(plan_ref[1] == k, info[blocks], bits)
    for b, (k, at) in enumerate(slots):
        meta_ref[b] = infos[k][plan_ref[2 + 2 * total + at]]
        meta_ref[blocks + b] = plan_ref[2 + total + at]
    meta_ref[2 * blocks] = bits
    meta_ref[2 * blocks + 1] = sub_ref[0]


def make_meta(slots, total, plan, sub, infos):
    blocks = len(slots)
    return pl.pallas_call(
        functools.partial(meta_kernel, slots, total),
        out_shape=jax.ShapeDtypeStruct((2 * blocks + 2,), jnp.int32),
        in_specs=[SMEM] * (2 + len(infos)),
        out_specs=SMEM,
        name="block_meta",
    )(plan, sub, *infos)


def score_kernel(blocks, rows, width, pieces, owned, runs, steps, first, outs, meta_ref, *refs):
    refs = list(refs)
    left_in = [refs.pop(0) for _ in owned]
    right_in = [refs.pop(0) for _ in range(2 * len(runs))]
    acc_in = None if first else refs.pop(0)
    out_refs = [refs.pop(0) for _ in (outs or (0,))]
    left, right, acc, left_scale, gram, left_sems, right_sems = refs
    per = pieces // 2
    copies = []
    for i, a in enumerate(owned):
        copies.append(pltpu.make_async_copy(left_in[i], left.at[pl.ds(a * rows, rows)], left_sems.at[i]))
    for i in range(2 * len(runs)):
        copies.append(pltpu.make_async_copy(right_in[i], right.at[i], right_sems.at[i]))
    for copy in copies:
        copy.start()
    eye = lax.broadcasted_iota(jnp.int32, (rows, rows), 0) == lax.broadcasted_iota(jnp.int32, (rows, rows), 1)
    column = lax.broadcasted_iota(jnp.int32, (1, rows), 1)
    row = lax.broadcasted_iota(jnp.int32, (rows, 1), 0)
    sub = meta_ref[2 * blocks + 1]
    bits = meta_ref[2 * blocks]

    def squares(block):
        wide = block.astype(jnp.float32)
        return jnp.sum(wide * wide, axis=1, keepdims=True)

    def lanes(col):
        return jnp.sum(jnp.where(eye, col, 0.0), axis=0, keepdims=True)

    if first:
        acc[...] = jnp.zeros_like(acc)
    else:
        acc[...] = acc_in[...]
    for i, a in enumerate(owned):
        copies[i].wait()

    @pl.loop(0, len(owned))
    def _(i):
        here = pl.ds((owned[0] + i) * rows, rows)
        inv = lax.rsqrt(squares(left[here, :]) * (1.0 / width) + norm_eps)
        left_scale[here, :] = jnp.broadcast_to(inv * (kernel_scale / width * math.log2(math.e)), (rows, rows))

    arrived = 0
    for lo, hi, start, end in steps:
        fresh = end > arrived

        @pl.loop(start, end)
        def _(run):
            if fresh:
                for h in range(2):
                    pltpu.make_async_copy(right_in[0], right.at[2 * run + h], right_sems.at[2 * run + h]).wait()
            flat = runs[0] + run
            b = lax.div(flat, per)
            q = 2 * lax.rem(flat, per)
            scale_row, valid = [], []
            for h in range(2):
                scale_row.append(lax.rsqrt(lanes(squares(right[2 * run + h])) * (1.0 / width) + norm_eps))
                valid.append((column + (sub ^ (q + h)) * rows < meta_ref[b]).astype(jnp.float32))
            both = jnp.concatenate([right[2 * run], right[2 * run + 1]], axis=0)
            gram[:(hi - lo) * rows, :] = lax.dot_general(
                left[lo * rows:hi * rows, :], both, (((1,), (1,)), ((), ())), preferred_element_type=jnp.float32)
            for a in range(lo, hi):
                here = slice(a * rows, (a + 1) * rows)
                there = slice((a - lo) * rows, (a - lo + 1) * rows)
                paired = (bits >> (meta_ref[blocks + a] * blocks + meta_ref[blocks + b])) & 1
                weight = paired.astype(jnp.float32)
                scale = left_scale[here, :]
                same = eye & ((b == a) & (q == 0))
                near = jnp.exp2(gram[there, :rows] * scale * scale_row[0]) * (valid[0] * weight)
                far = jnp.exp2(gram[there, rows:] * scale * scale_row[1]) * (valid[1] * weight)
                acc[here, :] += jnp.where(same, 0.0, near) + far

        arrived = max(arrived, end)
    if outs is None:
        out_refs[0][...] = acc[...]
        return
    for ref, group in zip(out_refs, outs):
        for n, a in enumerate(group):
            total = jnp.sum(acc[a * rows:(a + 1) * rows, :], axis=1, keepdims=True)
            total = jnp.where(row + sub * rows < meta_ref[a], total, 0.0)
            ref[n:n + 1, :] = jnp.log1p(lanes(total) / (pieces * rows))


def score(blocks, pieces, held, meta, owned, runs, steps, acc=None, outs=None, name="score"):
    rows, width = held[0, 0].shape
    per = pieces // 2
    rights = [held[run // per, 2 * (run % per) + h] for run in runs for h in range(2)]
    tall = max(hi - lo for lo, hi, _, _ in steps) * rows
    sums = jax.ShapeDtypeStruct((blocks * rows, rows), jnp.float32)
    out_shape = [sums] if outs is None else [jax.ShapeDtypeStruct((len(g), rows), jnp.float32) for g in outs]
    flops = sum(4 * (hi - lo) * (end - start) * rows * rows * width for lo, hi, start, end in steps)
    moved = (len(owned) + len(rights)) * rows * width * 2
    result = pl.pallas_call(
        functools.partial(score_kernel, blocks, rows, width, pieces, owned, runs, steps, acc is None, outs),
        out_shape=out_shape,
        in_specs=[SMEM] + [ANY] * (len(owned) + len(rights)) + ([] if acc is None else [VMEM]),
        out_specs=[VMEM] * len(out_shape),
        scratch_shapes=[
            pltpu.VMEM((blocks * rows, width), jnp.bfloat16),
            pltpu.VMEM((len(rights), rows, width), jnp.bfloat16),
            pltpu.VMEM((blocks * rows, rows), jnp.float32),
            pltpu.VMEM((blocks * rows, rows), jnp.float32),
            pltpu.VMEM((tall, 2 * rows), jnp.float32),
            pltpu.SemaphoreType.DMA((len(owned),)),
            pltpu.SemaphoreType.DMA((len(rights),)),
        ],
        compiler_params=pltpu.CompilerParams(vmem_limit_bytes=VMEM_LIMIT),
        cost_estimate=pl.CostEstimate(flops=flops, bytes_accessed=moved, transcendentals=0),
        name=name,
    )(meta, *[held[a, 0] for a in owned], *rights, *([] if acc is None else [acc]))
    return result[0] if outs is None else result


def place_kernel(slots, plan_ref, *refs):
    out_ref = refs[-1]
    for ref, (group) in zip(refs[:-1], slots):
        for n, at in enumerate(group):
            out_ref[pl.ds(plan_ref[2 + at], 1), :] = ref[n:n + 1, :]


def place_rows(slots, plan, returned, blocks, rows):
    return pl.pallas_call(
        functools.partial(place_kernel, slots),
        out_shape=jax.ShapeDtypeStruct((blocks, rows), jnp.float32),
        in_specs=[SMEM] + [VMEM] * len(returned),
        out_specs=VMEM,
        name="place_rows",
    )(plan, *returned)


def shift_by(array, k, places):
    return lax.ppermute(array, "blk", [(i, (i + k) % places) for i in range(places)])


def swap_with(array, q, pieces):
    return lax.ppermute(array, "sub", [(i, i ^ q) for i in range(pieces)])


def pattern_path(counts, capacity, pieces, sub, plan, info, slots):
    places = len(counts)
    order = sorted((k for k in range(places) if counts[k]), key=lambda k: (k * (places - k), k))
    taken = [(k, k * capacity + j) for k in order for j in range(counts[k])]
    blocks = len(taken)
    rows = slots[0].shape[0]
    infos = [info if k == 0 else shift_by(info, k, places) for k in range(places)]
    meta = make_meta(taken, places * capacity, plan, sub, infos)
    held = {}
    for b, (k, at) in enumerate(taken):
        held[b, 0] = slots[at] if k == 0 else shift_by(slots[at], k, places)
    for b in range(blocks):
        held[b, 2] = swap_with(held[b, 0], 2, pieces)
        held[b, 1] = swap_with(held[b, 0], 1, pieces)
        held[b, 3] = swap_with(held[b, 2], 1, pieces)
    end = blocks - 1
    per = pieces // 2
    early = range(end * per)
    acc = score(blocks, pieces, held, meta, range(end), early, [(0, end, 0, len(early))], name="score_early")
    most = range(end * per + per - 1)
    acc = score(blocks, pieces, held, meta, range(blocks), most,
                [(end, blocks, 0, len(early)), (0, blocks, len(early), len(most))], acc, name="score_middle")
    groups = [[b for b in range(blocks) if taken[b][0] == k] for k in order]
    sums = score(blocks, pieces, held, meta, range(blocks), range(len(most), blocks * per), [(0, blocks, 0, 1)], acc, groups,
                 name="score_late")
    returned = [s if k == 0 else shift_by(s, places - k, places) for k, s in zip(order, sums)]
    return place_rows([[taken[b][1] for b in g] for g in groups], plan, returned, blocks, rows)


def general_path(capacity, pieces, embeddings, row_count, fetch_list, left, right, pairs):
    places = lax.axis_size("blk")
    me = lax.axis_index("blk")
    sub = lax.axis_index("sub")
    blocks, rows, width = embeddings.shape
    total = places * capacity
    local_ids = jnp.arange(blocks, dtype=jnp.int32)
    slot_ids = jnp.arange(total, dtype=jnp.int32)
    owned = me * blocks + local_ids
    here = fetch_list[:, :, None] == owned[None, None, :]
    scorer = jnp.sum(jnp.where(here, jnp.arange(places, dtype=jnp.int32)[:, None, None], 0), axis=(0, 1))
    same = scorer[:, None] == scorer[None, :]
    rank = jnp.sum(same & (local_ids[None, :] < local_ids[:, None]), axis=1)
    send_slot = scorer * capacity + rank
    placing = send_slot[:, None] == slot_ids[None, :]
    source = jnp.sum(jnp.where(placing, local_ids[:, None], 0), axis=0)
    out_counts = jnp.where(jnp.any(placing, axis=0), jnp.take(row_count, source), 0)
    exchange = lambda x: lax.all_to_all(x, "blk", split_axis=0, concat_axis=0, tiled=True)
    incoming = exchange(jnp.take(embeddings, source, axis=0))
    in_counts = exchange(out_counts)
    wanted = lax.dynamic_index_in_dim(fetch_list, me, 0, keepdims=False)
    owner, local = wanted // blocks, wanted % blocks
    together = owner[:, None] == owner[None, :]
    recv_rank = jnp.sum(together & (local[None, :] < local[:, None]), axis=1)
    recv_slot = owner * capacity + recv_rank
    counts = jnp.take(in_counts, recv_slot, axis=0)
    live = jnp.arange(left.shape[1], dtype=jnp.int32) < pairs[0]
    one = jnp.int32(1)
    hot = lambda at: jnp.where(live[:, None], (at[:, None] == jnp.arange(blocks * blocks)).astype(jnp.int32), 0)
    listed = jnp.max(hot(left[0] * blocks + right[0]) | hot(right[0] * blocks + left[0]), axis=0)
    bits = jnp.sum(listed * lax.shift_left(one, jnp.arange(blocks * blocks, dtype=jnp.int32)))
    meta = jnp.concatenate([counts, local_ids, bits[None], sub[None].astype(jnp.int32)]).astype(jnp.int32)
    held = {}
    for b in range(blocks):
        held[b, 0] = lax.dynamic_index_in_dim(incoming, recv_slot[b], 0, keepdims=False)
        for q in range(1, pieces):
            held[b, q] = swap_with(held[b, 0], q, pieces)
    runs = range(blocks * pieces // 2)
    (dense,) = score(blocks, pieces, held, meta, range(blocks), runs, [(0, blocks, 0, len(runs))], None,
                     [list(range(blocks))], name="score_all")
    back = (recv_slot[None, :] == slot_ids[:, None]).astype(jnp.float32)
    returned = exchange(jnp.sum(back[:, :, None] * dense[None, :, :], axis=1))
    return jnp.take(returned, send_slot, axis=0)


def body(embeddings, row_count, fetch_list, pair_left, pair_right, pair_count):
    places = lax.axis_size("blk")
    pieces = lax.axis_size("sub")
    blocks = embeddings.shape[0]
    capacity = (blocks + places - 1) // places
    given = (embeddings, row_count, fetch_list, pair_left, pair_right, pair_count)
    general = functools.partial(general_path, capacity, pieces)
    patterns = block_patterns(places, capacity, blocks)
    if not patterns or pieces != 4:
        return general(*given)
    me = lax.axis_index("blk").astype(jnp.int32)[None]
    sub = lax.axis_index("sub").astype(jnp.int32)[None]
    plan, info, slots = make_plan(patterns, places, capacity, me, *given)
    branches = [
        lambda plan, info, slots, given, counts=counts: pattern_path(counts, capacity, pieces, sub, plan, info, slots)
        for counts in patterns
    ] + [lambda plan, info, slots, given: general(*given)]
    return lax.switch(plan[0], branches, plan, info, slots, given)


def solution(mesh):
    in_specs = (
        P(("parts", "blk"), "sub", None),
        P(("parts", "blk")),
        P("parts", None),
        P(("parts", "blk"), None),
        P(("parts", "blk"), None),
        P(("parts", "blk")),
    )
    out_specs = P(("parts", "blk"), "sub")
    return jax.shard_map(body, mesh=mesh, in_specs=in_specs, out_specs=out_specs, check_vma=False)
```

```python
import functools
import itertools
import math

import jax
import jax.numpy as jnp
from jax import lax
from jax.experimental import pallas as pl
from jax.experimental.pallas import tpu as pltpu
from jax.sharding import PartitionSpec as P

kernel_scale = 24.0
norm_eps = 1e-06
LANES = 128
FLOPS = 4
UNUSED = 2.0 ** 60
UNUSED_SQUARES = 2.0 ** 100
SCALE_IN_USE = 2.0 ** -30
VMEM_LIMIT = 24 * 1024 * 1024
ANY = pl.BlockSpec(memory_space=pl.ANY)
SMEM = pl.BlockSpec(memory_space=pltpu.SMEM)
VMEM = pl.BlockSpec(memory_space=pltpu.VMEM)


def block_patterns(places, capacity, blocks):
    if capacity < 2 or places > 4:
        return []
    cost = lambda counts: sum(c * min(k, places - k) for k, c in enumerate(counts))
    best = {}
    for counts in itertools.product(range(capacity + 1), repeat=places):
        if sum(counts) != blocks:
            continue
        turns = [counts[t:] + counts[:t] for t in range(places)]
        pick = min(turns, key=lambda c: (cost(c), c))
        best[min(turns)] = pick
    return sorted(best.values(), key=cost)


def unary(counts):
    return sum(((1 << c) - 1) << (2 * r) for r, c in enumerate(counts))


def marked(first_lanes, sub, count):
    rows, lanes = first_lanes.shape
    row = lax.broadcasted_iota(jnp.int32, (rows, lanes), 0) + sub * rows
    lane = lax.broadcasted_iota(jnp.int32, (rows, lanes), 1)
    return jnp.where((row >= count) & (lane == 0), UNUSED, first_lanes.astype(jnp.float32)).astype(first_lanes.dtype)


def plan_kernel(patterns, places, capacity, me_ref, sub_ref, fetch_ref, count_ref, left_ref, right_ref, pairs_ref,
                emb_ref, plan_ref, bits_ref, *rest):
    slots, sems = rest[:-1], rest[-1]
    blocks = count_ref.shape[0]
    rows = emb_ref.shape[1]
    views = [slots[0].at[pl.ds(j * rows, rows)] for j in range(capacity)] + list(slots[1:])
    me = me_ref[0]
    used = jnp.int32(0)
    for s in range(places):
        seen = jnp.int32(0)
        for p in range(blocks):
            owner = lax.div(fetch_ref[s, p], blocks)
            bit = lax.shift_left(jnp.int32(1), 2 * lax.rem(owner + (places - s), places))
            seen = seen | bit | ((seen & bit) << 1)
        used = used | seen
    choice = jnp.int32(len(patterns))
    shift = jnp.int32(0)
    for m in reversed(range(len(patterns))):
        for t in range(places):
            allowed = unary([patterns[m][(t - r) % places] for r in range(places)])
            fits = (used & ~allowed) == 0
            choice = jnp.where(fits, m, choice)
            shift = jnp.where(fits, t, shift)
    plan_ref[0] = choice
    plan_ref[1] = shift
    mine = lax.rem(me + places - shift, places)
    total = places * capacity
    copies = []
    for k in range(places):
        owner = lax.rem(me + places - k, places)
        target = lax.rem(me + k + places - shift, places)
        place, lid, seen = [jnp.int32(0)] * capacity, [jnp.int32(0)] * capacity, jnp.int32(0)
        send, sent = [jnp.int32(0)] * capacity, jnp.int32(0)
        for p in range(blocks):
            listed = fetch_ref[mine, p]
            hit = lax.div(listed, blocks) == owner
            outward = fetch_ref[target, p]
            goes = lax.div(outward, blocks) == me
            for j in range(capacity):
                place[j] = jnp.where(hit & (seen == j), p, place[j])
                lid[j] = jnp.where(hit & (seen == j), listed - owner * blocks, lid[j])
                send[j] = jnp.where(goes & (sent == j), outward - me * blocks, send[j])
            seen = seen + hit.astype(jnp.int32)
            sent = sent + goes.astype(jnp.int32)
        for j in range(capacity):
            at = k * capacity + j
            copy = pltpu.make_async_copy(emb_ref.at[send[j]], views[at], sems.at[at])
            pl.when(sent > j)(copy.start)
            copies.append((sent > j, copy))
            plan_ref[2 + at] = send[j]
            plan_ref[2 + total + at] = place[j]
            plan_ref[2 + 2 * total + at] = lid[j]
    bits = jnp.int32(0)
    for p in range(left_ref.shape[1]):
        a, b = left_ref[0, p], right_ref[0, p]
        both = lax.shift_left(jnp.int32(1), a * blocks + b) | lax.shift_left(jnp.int32(1), b * blocks + a)
        bits = bits | jnp.where(p < pairs_ref[0], both, 0)
    bits_ref[0] = bits
    for at, (filled, copy) in enumerate(copies):
        pl.when(filled)(copy.wait)
        views[at][:, :LANES] = marked(views[at][:, :LANES], sub_ref[0], count_ref[plan_ref[2 + at]])


def make_plan(patterns, places, capacity, me, sub, embeddings, row_count, fetch_list, left, right, pairs):
    blocks, rows, width = embeddings.shape
    total = places * capacity
    slot = jax.ShapeDtypeStruct((rows, width), embeddings.dtype)
    own = jax.ShapeDtypeStruct((capacity * rows, width), embeddings.dtype)
    others = total - capacity
    out = pl.pallas_call(
        functools.partial(plan_kernel, patterns, places, capacity),
        out_shape=[jax.ShapeDtypeStruct((2 + 3 * total,), jnp.int32),
                   jax.ShapeDtypeStruct((1,), jnp.int32), own] + [slot] * others,
        in_specs=[SMEM] * 7 + [ANY],
        out_specs=[SMEM, SMEM] + [VMEM] * (1 + others),
        scratch_shapes=[pltpu.SemaphoreType.DMA((total,))],
        name="plan_and_gather",
    )(me, sub, fetch_list, row_count, left, right, pairs, embeddings)
    return out[0], out[1], out[2], out[3:]


def pairs_of(per, runs, steps):
    return [(a, b) for lo, hi, start, end in steps
            for b in sorted({runs[run] // per for run in range(start, end)}) for a in range(lo, hi)]


def score_kernel(rows, width, pieces, wheres, owned, runs, steps, places, *refs):
    refs = list(refs)
    arrays = [refs.pop(0) for _ in range(1 + max(i for i, _ in wheres))]
    spots_in = [arrays[i].at[pl.ds(n * rows, rows)] for i, n in wheres]
    left_in, right_in = spots_in[:len(owned)], spots_in[len(owned):]
    finish = None
    if places is not None:
        finish = [refs.pop(0) for _ in range(2 + places[0])]
    out_refs = [refs.pop(0) for _ in (places[2] if places else (0,))]
    left, right, left_scale, gram, left_sems, right_sems = refs[:6]
    sums = refs[6] if places else out_refs[0]
    per = pieces // 2
    copies = []
    for i, a in enumerate(owned):
        copies.append(pltpu.make_async_copy(left_in[i], left.at[pl.ds(a * rows, rows)], left_sems.at[i]))
    for i in range(2 * len(runs)):
        copies.append(pltpu.make_async_copy(right_in[i], right.at[pl.ds(i * rows, rows)], right_sems.at[i]))
    for copy in copies:
        copy.start()
    eye = lax.broadcasted_iota(jnp.int32, (rows, rows), 0) == lax.broadcasted_iota(jnp.int32, (rows, rows), 1)

    def squares(block):
        wide = block.astype(jnp.float32)
        return jnp.sum(wide * wide, axis=1, keepdims=True)

    def lanes(col):
        return jnp.sum(jnp.where(eye, col, 0.0), axis=0, keepdims=True)

    for i in range(len(owned)):
        copies[i].wait()

    @pl.loop(0, len(owned))
    def _(i):
        here = pl.ds((owned[0] + i) * rows, rows)
        inv = lax.rsqrt(squares(left[here, :]) * (1.0 / width) + norm_eps)
        left_scale[here, :] = jnp.broadcast_to(inv * (kernel_scale / width * math.log2(math.e)), (rows, rows))

    arrived = base = 0
    for lo, hi, start, end in steps:
        fresh = end > arrived
        first_block = runs[start] // per

        @pl.loop(start, end)
        def _(run):
            if fresh:
                for h in range(2):
                    pltpu.make_async_copy(
                        right_in[0], right.at[pl.ds((2 * run + h) * rows, rows)], right_sems.at[2 * run + h]).wait()
            flat = runs[0] + run
            b = lax.div(flat, per)
            q = 2 * lax.rem(flat, per)
            scale_row, valid = [], []
            for h in range(2):
                here = pl.ds(pl.multiple_of((2 * run + h) * rows, rows), rows)
                total = lanes(squares(right[here, :]))
                scale_row.append(lax.rsqrt(total * (1.0 / width) + norm_eps))
                valid.append((total < UNUSED_SQUARES).astype(jnp.float32))
            both = right[pl.ds(pl.multiple_of(2 * run * rows, rows), 2 * rows), :]
            gram[:(hi - lo) * rows, :] = lax.dot_general(
                left[lo * rows:hi * rows, :], both, (((1,), (1,)), ((), ())), preferred_element_type=jnp.float32)
            for a in range(lo, hi):
                there = slice((a - lo) * rows, (a - lo + 1) * rows)
                scale = left_scale[a * rows:(a + 1) * rows, :]
                same = eye & ((b == a) & (q == 0))
                near = jnp.exp2(gram[there, :rows] * scale * scale_row[0]) * valid[0]
                far = jnp.exp2(gram[there, rows:] * scale * scale_row[1]) * valid[1]
                tile = jnp.where(same, 0.0, near) + far
                pair = base + (b - first_block) * (hi - lo) + a - lo
                if end - start > 1:
                    tile = tile + jnp.where(q == 0, 0.0, sums[pair])
                sums[pair] = tile

        arrived = max(arrived, end)
        base += (runs[end - 1] // per + 1 - first_block) * (hi - lo)
    if places is None:
        return
    count, spots, groups, listed = places
    plan_ref, bits_ref = finish[:2]
    bits = bits_ref[0]
    spot = [plan_ref[at] for at in spots]
    blocks = len(spots)
    for ref, group in zip(out_refs, groups):
        for n, a in enumerate(group):
            total = jnp.zeros((rows, rows), jnp.float32)
            for source, at, right_block in listed[a]:
                paired = (bits >> (spot[a] * blocks + spot[right_block])) & 1
                total = total + (sums if source < 0 else finish[2 + source])[at] * paired.astype(jnp.float32)
            total = jnp.sum(total, axis=1, keepdims=True)
            total = jnp.where(left_scale[a * rows:(a + 1) * rows, :1] > SCALE_IN_USE, total, 0.0)
            ref[n:n + 1, :] = jnp.log1p(lanes(total) / (pieces * rows))


def score(pieces, held, owned, runs, steps, meta=None, name="score"):
    width = held[owned[0], 0][0].shape[1]
    rows = held[owned[0], 0][2]
    per = pieces // 2
    rights = [held[run // per, 2 * (run % per) + h] for run in runs for h in range(2)]
    arrays, wheres = [], []
    for array, n, _ in [held[a, 0] for a in owned] + rights:
        known = [i for i, other in enumerate(arrays) if other is array]
        if not known:
            arrays.append(array)
        wheres.append((known[0] if known else len(arrays) - 1, n))
    tall = max(hi - lo for lo, hi, _, _ in steps) * rows
    pairs = pairs_of(per, runs, steps)
    sums = jax.ShapeDtypeStruct((len(pairs), rows, rows), jnp.float32)
    places, extra, extra_specs, out_shape, scratch = None, [], [], [sums], []
    if meta is not None:
        plan, spots, bits, groups, earlier = meta
        listed = [[] for _ in spots]
        for source, (_, known) in enumerate(earlier + [(None, pairs)]):
            for at, (a, b) in enumerate(known):
                listed[a].append((source if source < len(earlier) else -1, at, b))
        places = len(earlier), spots, groups, listed
        extra = [plan, bits] + [array for array, _ in earlier]
        extra_specs = [SMEM, SMEM] + [VMEM] * len(earlier)
        out_shape = [jax.ShapeDtypeStruct((len(g), rows), jnp.float32) for g in groups]
        scratch = [pltpu.VMEM(sums.shape, jnp.float32)]
    flops = sum(4 * (hi - lo) * (end - start) * rows * rows * width for lo, hi, start, end in steps)
    moved = (len(owned) + len(rights)) * rows * width * 2
    result = pl.pallas_call(
        functools.partial(score_kernel, rows, width, pieces, wheres, owned, runs, steps, places),
        out_shape=out_shape,
        in_specs=[ANY] * len(arrays) + extra_specs,
        out_specs=[VMEM] * len(out_shape),
        scratch_shapes=[
            pltpu.VMEM((owned[-1] * rows + rows, width), jnp.bfloat16),
            pltpu.VMEM((len(rights) * rows, width), jnp.bfloat16),
            pltpu.VMEM((owned[-1] * rows + rows, rows), jnp.float32),
            pltpu.VMEM((tall, 2 * rows), jnp.float32),
            pltpu.SemaphoreType.DMA((len(owned),)),
            pltpu.SemaphoreType.DMA((len(rights),)),
        ] + scratch,
        compiler_params=pltpu.CompilerParams(vmem_limit_bytes=VMEM_LIMIT),
        cost_estimate=pl.CostEstimate(flops=FLOPS * flops, bytes_accessed=moved, transcendentals=0),
        name=name,
    )(*arrays, *extra)
    return (result[0], pairs) if meta is None else result


def place_kernel(slots, plan_ref, *refs):
    out_ref = refs[-1]
    for ref, (group) in zip(refs[:-1], slots):
        for n, at in enumerate(group):
            out_ref[pl.ds(plan_ref[2 + at], 1), :] = ref[n:n + 1, :]


def place_rows(slots, plan, returned, blocks, rows):
    return pl.pallas_call(
        functools.partial(place_kernel, slots),
        out_shape=jax.ShapeDtypeStruct((blocks, rows), jnp.float32),
        in_specs=[SMEM] + [VMEM] * len(returned),
        out_specs=VMEM,
        name="place_rows",
    )(plan, *returned)


def shift_by(array, k, places):
    return lax.ppermute(array, "blk", [(i, (i + k) % places) for i in range(places)])


def swap_with(array, q, pieces):
    return lax.ppermute(array, "sub", [(i, i ^ q) for i in range(pieces)])


def after(array, *others):
    return lax.optimization_barrier((array,) + others)[0]


def pattern_path(counts, capacity, pieces, rows, plan, bits, own, slots):
    places = len(counts)
    nearest = sorted((k for k in range(1, places) if counts[k]), key=lambda k: min(k, places - k))
    sets = [[(0, j) for j in range(counts[0])], [(k, 0) for k in nearest[:2]],
            [(k, 0) for k in nearest[2:]] + [(k, 1) for k in nearest if counts[k] > 1]]
    taken = [(k, k * capacity + j) for group in sets for k, j in group]
    blocks = len(taken)
    per = pieces // 2
    sends = [lambda x: x] + [functools.partial(shift_by, k=k, places=places) for k in range(1, places)]
    moved = [shift_by(slots[at - capacity], k, places) for k, at in taken if k]
    here = lax.switch(plan[1], sends, after(bits, moved[0]))
    arrived = [own if len(sets[0]) == capacity else own[:rows], jnp.concatenate(moved[:2], axis=0),
               moved[2] if len(moved) == 3 else jnp.concatenate(moved[2:], axis=0)]
    held = {}
    first = [0, len(sets[0]), len(sets[0]) + 2, blocks]
    ready, end = first[1], first[2]
    for g, array in enumerate(arrived):
        across = swap_with(array, 2, pieces)
        beside = swap_with(array, 1, pieces)
        if g == 2:
            near = score(pieces, held, range(end), range(ready * per, end * per), [(0, end, 0, (end - ready) * per)],
                         name="score_near")
        for n, b in enumerate(range(first[g], first[g + 1])):
            held[b, 0], held[b, 1], held[b, 2] = (array, n, rows), (beside, n, rows), (across, n, rows)
        if g == 1:
            early = score(pieces, held, range(end), range(ready * per), [(0, end, 0, ready * per)], name="score_early")
        if g == 2:
            steps = [(end, blocks, 0, end * per)]
            runs = range(end * per)
            if blocks - end == 1:
                runs = range(end * per + per - 1)
                steps.append((0, blocks, end * per, len(runs)))
            far = score(pieces, held, range(blocks), runs, steps, name="score_far")
            across = after(across, early[0], near[0], far[0], here)
        corner = swap_with(across, 1, pieces)
        for n, b in enumerate(range(first[g], first[g + 1])):
            held[b, 3] = (corner, n, rows)
    order = sorted({k for k, _ in taken})
    groups = [[b for b in range(blocks) if taken[b][0] == k] for k in order]
    sums = score(pieces, held, range(blocks), range(len(runs), blocks * per), [(0, blocks, 0, blocks * per - len(runs))],
                 (plan, [2 + places * capacity + at for _, at in taken], here, groups, [early, near, far]), name="score_late")
    returned = [s if k == 0 else shift_by(s, places - k, places) for k, s in zip(order, sums)]
    return place_rows([[taken[b][1] for b in g] for g in groups], plan, returned, blocks, rows)


def general_path(capacity, pieces, embeddings, row_count, fetch_list, left, right, pairs):
    places = lax.axis_size("blk")
    me = lax.axis_index("blk")
    sub = lax.axis_index("sub")
    blocks, rows, width = embeddings.shape
    total = places * capacity
    local_ids = jnp.arange(blocks, dtype=jnp.int32)
    slot_ids = jnp.arange(total, dtype=jnp.int32)
    owned = me * blocks + local_ids
    here = fetch_list[:, :, None] == owned[None, None, :]
    scorer = jnp.sum(jnp.where(here, jnp.arange(places, dtype=jnp.int32)[:, None, None], 0), axis=(0, 1))
    same = scorer[:, None] == scorer[None, :]
    rank = jnp.sum(same & (local_ids[None, :] < local_ids[:, None]), axis=1)
    send_slot = scorer * capacity + rank
    placing = send_slot[:, None] == slot_ids[None, :]
    source = jnp.sum(jnp.where(placing, local_ids[:, None], 0), axis=0)
    exchange = lambda x: lax.all_to_all(x, "blk", split_axis=0, concat_axis=0, tiled=True)
    mark = jax.vmap(lambda block, count: block.at[:, :LANES].set(marked(block[:, :LANES], sub, count)))
    incoming = exchange(jnp.take(mark(embeddings, row_count), source, axis=0))
    wanted = lax.dynamic_index_in_dim(fetch_list, me, 0, keepdims=False)
    owner, local = wanted // blocks, wanted % blocks
    together = owner[:, None] == owner[None, :]
    recv_rank = jnp.sum(together & (local[None, :] < local[:, None]), axis=1)
    recv_slot = owner * capacity + recv_rank
    live = jnp.arange(left.shape[1], dtype=jnp.int32) < pairs[0]
    one = jnp.int32(1)
    hot = lambda at: jnp.where(live[:, None], (at[:, None] == jnp.arange(blocks * blocks)).astype(jnp.int32), 0)
    listed = jnp.max(hot(left[0] * blocks + right[0]) | hot(right[0] * blocks + left[0]), axis=0)
    bits = jnp.sum(listed * lax.shift_left(one, jnp.arange(blocks * blocks, dtype=jnp.int32)))
    held = {}
    for b in range(blocks):
        block = lax.dynamic_index_in_dim(incoming, recv_slot[b], 0, keepdims=False)
        for q in range(pieces):
            held[b, q] = (swap_with(block, q, pieces) if q else block), 0, rows
    runs = range(blocks * pieces // 2)
    meta = local_ids, range(blocks), bits[None].astype(jnp.int32), [list(range(blocks))], []
    (dense,) = score(pieces, held, range(blocks), runs, [(0, blocks, 0, len(runs))], meta, name="score_all")
    back = (recv_slot[None, :] == slot_ids[:, None]).astype(jnp.float32)
    returned = exchange(jnp.sum(back[:, :, None] * dense[None, :, :], axis=1))
    return jnp.take(returned, send_slot, axis=0)


def body(embeddings, row_count, fetch_list, pair_left, pair_right, pair_count):
    places = lax.axis_size("blk")
    pieces = lax.axis_size("sub")
    blocks = embeddings.shape[0]
    capacity = (blocks + places - 1) // places
    given = (embeddings, row_count, fetch_list, pair_left, pair_right, pair_count)
    general = functools.partial(general_path, capacity, pieces)
    patterns = block_patterns(places, capacity, blocks)
    if not patterns or pieces != 4:
        return general(*given)
    me = lax.axis_index("blk").astype(jnp.int32)[None]
    sub = lax.axis_index("sub").astype(jnp.int32)[None]
    plan, bits, own, slots = make_plan(patterns, places, capacity, me, sub, *given)
    rows = embeddings.shape[1]
    branches = [
        lambda plan, bits, own, slots, given, counts=counts: pattern_path(counts, capacity, pieces, rows, plan, bits, own, slots)
        for counts in patterns
    ] + [lambda plan, bits, own, slots, given: general(*given)]
    return lax.switch(plan[0], branches, plan, bits, own, slots, given)


def solution(mesh):
    in_specs = (
        P(("parts", "blk"), "sub", None),
        P(("parts", "blk")),
        P("parts", None),
        P(("parts", "blk"), None),
        P(("parts", "blk"), None),
        P(("parts", "blk")),
    )
    out_specs = P(("parts", "blk"), "sub")
    return jax.shard_map(body, mesh=mesh, in_specs=in_specs, out_specs=out_specs, check_vma=False)
```

```python
import functools
import itertools
import math

import jax
import jax.numpy as jnp
from jax import lax
from jax.experimental import pallas as pl
from jax.experimental.pallas import tpu as pltpu
from jax.sharding import PartitionSpec as P

kernel_scale = 24.0
norm_eps = 1e-06
LANES = 128
FLOPS = 4
UNUSED = 2.0 ** 60
UNUSED_SQUARES = 2.0 ** 100
SCALE_IN_USE = 2.0 ** -30
VMEM_LIMIT = 24 * 1024 * 1024
ANY = pl.BlockSpec(memory_space=pl.ANY)
SMEM = pl.BlockSpec(memory_space=pltpu.SMEM)
VMEM = pl.BlockSpec(memory_space=pltpu.VMEM)


def block_patterns(places, capacity, blocks):
    if capacity < 2 or places > 4:
        return []
    cost = lambda counts: sum(c * min(k, places - k) for k, c in enumerate(counts))
    best = {}
    for counts in itertools.product(range(capacity + 1), repeat=places):
        if sum(counts) != blocks:
            continue
        turns = [counts[t:] + counts[:t] for t in range(places)]
        pick = min(turns, key=lambda c: (-c[0], cost(c), c))
        best[min(turns)] = pick
    return sorted(best.values(), key=cost)


def unary(counts):
    return sum(((1 << c) - 1) << (2 * r) for r, c in enumerate(counts))


def marked(first_lanes, sub, count):
    rows, lanes = first_lanes.shape
    row = lax.broadcasted_iota(jnp.int32, (rows, lanes), 0) + sub * rows
    lane = lax.broadcasted_iota(jnp.int32, (rows, lanes), 1)
    return jnp.where((row >= count) & (lane == 0), UNUSED, first_lanes.astype(jnp.float32)).astype(first_lanes.dtype)


def plan_kernel(patterns, places, capacity, me_ref, sub_ref, fetch_ref, count_ref, left_ref, right_ref, pairs_ref,
                emb_ref, plan_ref, bits_ref, *rest):
    slots, sems = rest[:-1], rest[-1]
    blocks = count_ref.shape[0]
    rows = emb_ref.shape[1]
    views = [slots[0].at[pl.ds(j * rows, rows)] for j in range(capacity)] + list(slots[1:])
    me = me_ref[0]
    used = jnp.int32(0)
    for s in range(places):
        seen = jnp.int32(0)
        for p in range(blocks):
            owner = lax.div(fetch_ref[s, p], blocks)
            bit = lax.shift_left(jnp.int32(1), 2 * lax.rem(owner + (places - s), places))
            seen = seen | bit | ((seen & bit) << 1)
        used = used | seen
    choice = jnp.int32(len(patterns))
    shift = jnp.int32(0)
    for m in reversed(range(len(patterns))):
        for t in range(places):
            allowed = unary([patterns[m][(t - r) % places] for r in range(places)])
            fits = (used & ~allowed) == 0
            choice = jnp.where(fits, m, choice)
            shift = jnp.where(fits, t, shift)
    plan_ref[0] = choice
    plan_ref[1] = shift
    mine = lax.rem(me + places - shift, places)
    total = places * capacity
    copies = []
    for k in range(places):
        owner = lax.rem(me + places - k, places)
        target = lax.rem(me + k + places - shift, places)
        place, lid, seen = [jnp.int32(0)] * capacity, [jnp.int32(0)] * capacity, jnp.int32(0)
        send, sent = [jnp.int32(0)] * capacity, jnp.int32(0)
        for p in range(blocks):
            listed = fetch_ref[mine, p]
            hit = lax.div(listed, blocks) == owner
            outward = fetch_ref[target, p]
            goes = lax.div(outward, blocks) == me
            for j in range(capacity):
                place[j] = jnp.where(hit & (seen == j), p, place[j])
                lid[j] = jnp.where(hit & (seen == j), listed - owner * blocks, lid[j])
                send[j] = jnp.where(goes & (sent == j), outward - me * blocks, send[j])
            seen = seen + hit.astype(jnp.int32)
            sent = sent + goes.astype(jnp.int32)
        for j in range(capacity):
            at = k * capacity + j
            copy = pltpu.make_async_copy(emb_ref.at[send[j]], views[at], sems.at[at])
            pl.when(sent > j)(copy.start)
            copies.append((sent > j, copy))
            plan_ref[2 + at] = send[j]
            plan_ref[2 + total + at] = place[j]
            plan_ref[2 + 2 * total + at] = lid[j]
    bits = jnp.int32(0)
    for p in range(left_ref.shape[1]):
        a, b = left_ref[0, p], right_ref[0, p]
        both = lax.shift_left(jnp.int32(1), a * blocks + b) | lax.shift_left(jnp.int32(1), b * blocks + a)
        bits = bits | jnp.where(p < pairs_ref[0], both, 0)
    bits_ref[0] = bits
    for at, (filled, copy) in enumerate(copies):
        pl.when(filled)(copy.wait)
        views[at][:, :LANES] = marked(views[at][:, :LANES], sub_ref[0], count_ref[plan_ref[2 + at]])


def make_plan(patterns, places, capacity, me, sub, embeddings, row_count, fetch_list, left, right, pairs):
    blocks, rows, width = embeddings.shape
    total = places * capacity
    slot = jax.ShapeDtypeStruct((rows, width), embeddings.dtype)
    own = jax.ShapeDtypeStruct((capacity * rows, width), embeddings.dtype)
    others = total - capacity
    out = pl.pallas_call(
        functools.partial(plan_kernel, patterns, places, capacity),
        out_shape=[jax.ShapeDtypeStruct((2 + 3 * total,), jnp.int32),
                   jax.ShapeDtypeStruct((1,), jnp.int32), own] + [slot] * others,
        in_specs=[SMEM] * 7 + [ANY],
        out_specs=[SMEM, SMEM] + [VMEM] * (1 + others),
        scratch_shapes=[pltpu.SemaphoreType.DMA((total,))],
        name="plan_and_gather",
    )(me, sub, fetch_list, row_count, left, right, pairs, embeddings)
    return out[0], out[1], out[2], out[3:]


def pairs_of(per, runs, steps):
    return [(a, b) for lo, hi, start, end in steps
            for b in sorted({runs[run] // per for run in range(start, end)}) for a in range(lo, hi)]


def score_kernel(rows, width, pieces, wheres, owned, runs, steps, places, *refs):
    refs = list(refs)
    arrays = [refs.pop(0) for _ in range(1 + max(i for i, _ in wheres))]
    spots_in = [arrays[i].at[pl.ds(n * rows, rows)] for i, n in wheres]
    left_in, right_in = spots_in[:len(owned)], spots_in[len(owned):]
    finish = None
    if places is not None:
        finish = [refs.pop(0) for _ in range(2 + places[0])]
    out_refs = [refs.pop(0) for _ in (places[2] if places else (0,))]
    left, right, left_scale, gram, left_sems, right_sems = refs[:6]
    sums = refs[6] if places else out_refs[0]
    per = pieces // 2
    copies = []
    for i, a in enumerate(owned):
        copies.append(pltpu.make_async_copy(left_in[i], left.at[pl.ds(a * rows, rows)], left_sems.at[i]))
    for i in range(2 * len(runs)):
        copies.append(pltpu.make_async_copy(right_in[i], right.at[pl.ds(i * rows, rows)], right_sems.at[i]))
    for copy in copies:
        copy.start()
    eye = lax.broadcasted_iota(jnp.int32, (rows, rows), 0) == lax.broadcasted_iota(jnp.int32, (rows, rows), 1)

    def squares(block):
        wide = block.astype(jnp.float32)
        return jnp.sum(wide * wide, axis=1, keepdims=True)

    def lanes(col):
        return jnp.sum(jnp.where(eye, col, 0.0), axis=0, keepdims=True)

    for i in range(len(owned)):
        copies[i].wait()

    @pl.loop(0, len(owned))
    def _(i):
        here = pl.ds((owned[0] + i) * rows, rows)
        inv = lax.rsqrt(squares(left[here, :]) * (1.0 / width) + norm_eps)
        left_scale[here, :] = jnp.broadcast_to(inv * (kernel_scale / width * math.log2(math.e)), (rows, rows))

    arrived = base = 0
    for lo, hi, start, end in steps:
        fresh = end > arrived
        first_block = runs[start] // per

        @pl.loop(start, end)
        def _(run):
            if fresh:
                for h in range(2):
                    pltpu.make_async_copy(
                        right_in[0], right.at[pl.ds((2 * run + h) * rows, rows)], right_sems.at[2 * run + h]).wait()
            flat = runs[0] + run
            b = lax.div(flat, per)
            q = 2 * lax.rem(flat, per)
            scale_row, valid = [], []
            for h in range(2):
                here = pl.ds(pl.multiple_of((2 * run + h) * rows, rows), rows)
                total = lanes(squares(right[here, :]))
                scale_row.append(lax.rsqrt(total * (1.0 / width) + norm_eps))
                valid.append((total < UNUSED_SQUARES).astype(jnp.float32))
            both = right[pl.ds(pl.multiple_of(2 * run * rows, rows), 2 * rows), :]
            gram[:(hi - lo) * rows, :] = lax.dot_general(
                left[lo * rows:hi * rows, :], both, (((1,), (1,)), ((), ())), preferred_element_type=jnp.float32)
            for a in range(lo, hi):
                there = slice((a - lo) * rows, (a - lo + 1) * rows)
                scale = left_scale[a * rows:(a + 1) * rows, :]
                same = eye & ((b == a) & (q == 0))
                near = jnp.exp2(gram[there, :rows] * scale * scale_row[0]) * valid[0]
                far = jnp.exp2(gram[there, rows:] * scale * scale_row[1]) * valid[1]
                tile = jnp.where(same, 0.0, near) + far
                pair = base + (b - first_block) * (hi - lo) + a - lo
                if end - start > 1:
                    tile = tile + jnp.where(q == 0, 0.0, sums[pair])
                sums[pair] = tile

        arrived = max(arrived, end)
        base += (runs[end - 1] // per + 1 - first_block) * (hi - lo)
    if places is None:
        return
    count, spots, groups, listed = places
    plan_ref, bits_ref = finish[:2]
    bits = bits_ref[0]
    spot = [plan_ref[at] for at in spots]
    blocks = len(spots)
    for ref, group in zip(out_refs, groups):
        for n, a in enumerate(group):
            total = jnp.zeros((rows, rows), jnp.float32)
            for source, at, right_block in listed[a]:
                paired = (bits >> (spot[a] * blocks + spot[right_block])) & 1
                total = total + (sums if source < 0 else finish[2 + source])[at] * paired.astype(jnp.float32)
            total = jnp.sum(total, axis=1, keepdims=True)
            total = jnp.where(left_scale[a * rows:(a + 1) * rows, :1] > SCALE_IN_USE, total, 0.0)
            ref[n:n + 1, :] = jnp.log1p(lanes(total) / (pieces * rows))


def score(pieces, held, owned, runs, steps, meta=None, name="score"):
    width = held[owned[0], 0][0].shape[1]
    rows = held[owned[0], 0][2]
    per = pieces // 2
    rights = [held[run // per, 2 * (run % per) + h] for run in runs for h in range(2)]
    arrays, wheres = [], []
    for array, n, _ in [held[a, 0] for a in owned] + rights:
        known = [i for i, other in enumerate(arrays) if other is array]
        if not known:
            arrays.append(array)
        wheres.append((known[0] if known else len(arrays) - 1, n))
    tall = max(hi - lo for lo, hi, _, _ in steps) * rows
    pairs = pairs_of(per, runs, steps)
    sums = jax.ShapeDtypeStruct((len(pairs), rows, rows), jnp.float32)
    places, extra, extra_specs, out_shape, scratch = None, [], [], [sums], []
    if meta is not None:
        plan, spots, bits, groups, earlier = meta
        listed = [[] for _ in spots]
        for source, (_, known) in enumerate(earlier + [(None, pairs)]):
            for at, (a, b) in enumerate(known):
                listed[a].append((source if source < len(earlier) else -1, at, b))
        places = len(earlier), spots, groups, listed
        extra = [plan, bits] + [array for array, _ in earlier]
        extra_specs = [SMEM, SMEM] + [VMEM] * len(earlier)
        out_shape = [jax.ShapeDtypeStruct((len(g), rows), jnp.float32) for g in groups]
        scratch = [pltpu.VMEM(sums.shape, jnp.float32)]
    flops = sum(4 * (hi - lo) * (end - start) * rows * rows * width for lo, hi, start, end in steps)
    moved = (len(owned) + len(rights)) * rows * width * 2
    result = pl.pallas_call(
        functools.partial(score_kernel, rows, width, pieces, wheres, owned, runs, steps, places),
        out_shape=out_shape,
        in_specs=[ANY] * len(arrays) + extra_specs,
        out_specs=[VMEM] * len(out_shape),
        scratch_shapes=[
            pltpu.VMEM((owned[-1] * rows + rows, width), jnp.bfloat16),
            pltpu.VMEM((len(rights) * rows, width), jnp.bfloat16),
            pltpu.VMEM((owned[-1] * rows + rows, rows), jnp.float32),
            pltpu.VMEM((tall, 2 * rows), jnp.float32),
            pltpu.SemaphoreType.DMA((len(owned),)),
            pltpu.SemaphoreType.DMA((len(rights),)),
        ] + scratch,
        compiler_params=pltpu.CompilerParams(vmem_limit_bytes=VMEM_LIMIT),
        cost_estimate=pl.CostEstimate(flops=FLOPS * flops, bytes_accessed=moved, transcendentals=0),
        name=name,
    )(*arrays, *extra)
    return (result[0], pairs) if meta is None else result


def place_kernel(slots, plan_ref, *refs):
    out_ref = refs[-1]
    for ref, (group) in zip(refs[:-1], slots):
        for n, at in enumerate(group):
            out_ref[pl.ds(plan_ref[2 + at], 1), :] = ref[n:n + 1, :]


def place_rows(slots, plan, returned, blocks, rows):
    return pl.pallas_call(
        functools.partial(place_kernel, slots),
        out_shape=jax.ShapeDtypeStruct((blocks, rows), jnp.float32),
        in_specs=[SMEM] + [VMEM] * len(returned),
        out_specs=VMEM,
        name="place_rows",
    )(plan, *returned)


def shift_by(array, k, places):
    return lax.ppermute(array, "blk", [(i, (i + k) % places) for i in range(places)])


def swap_with(array, q, pieces):
    return lax.ppermute(array, "sub", [(i, i ^ q) for i in range(pieces)])


def after(array, *others):
    return lax.optimization_barrier((array,) + others)[0]


def pattern_path(counts, capacity, pieces, rows, plan, bits, own, slots):
    places = len(counts)
    nearest = sorted((k for k in range(1, places) if counts[k]), key=lambda k: min(k, places - k))
    sets = [[(0, j) for j in range(counts[0])], [(nearest[0], 0)], [(nearest[1], 0)],
            [(k, 0) for k in nearest[2:]] + [(k, 1) for k in nearest if counts[k] > 1]]
    taken = [(k, k * capacity + j) for group in sets for k, j in group]
    blocks = len(taken)
    per = pieces // 2
    sends = [lambda x: x] + [functools.partial(shift_by, k=k, places=places) for k in range(1, places)]
    moved = [shift_by(slots[at - capacity], k, places) for k, at in taken if k]
    arrived = [own if len(sets[0]) == capacity else own[:rows], moved[0], moved[1],
               moved[2] if len(moved) == 3 else jnp.concatenate(moved[2:], axis=0)]
    held = {}
    first = [0, len(sets[0]), len(sets[0]) + 1, len(sets[0]) + 2, blocks]
    ready, end = first[1], first[3]
    acrosses = []
    for g, array in enumerate(arrived):
        across = swap_with(array, 2, pieces)
        acrosses.append(across)
        if g == 1:
            here = lax.switch(plan[1], sends, after(bits, across))
        beside = swap_with(array, 1, pieces)
        for n, b in enumerate(range(first[g], first[g + 1])):
            held[b, 0], held[b, 1], held[b, 2] = (array, n, rows), (beside, n, rows), (across, n, rows)
        if g == 3:
            runs = range(end * per + (per - 1) * (blocks - end == 1))
            most = score(pieces, held, range(blocks), runs, [(0, blocks, 0, len(runs))], name="score_most")
            across = after(across, most[0], here)
        corner = swap_with(across, 1, pieces)
        for n, b in enumerate(range(first[g], first[g + 1])):
            held[b, 3] = (corner, n, rows)
    order = sorted({k for k, _ in taken})
    groups = [[b for b in range(blocks) if taken[b][0] == k] for k in order]
    sums = score(pieces, held, range(blocks), range(len(runs), blocks * per), [(0, blocks, 0, blocks * per - len(runs))],
                 (plan, [2 + places * capacity + at for _, at in taken], here, groups, [most]), name="score_late")
    returned = [s if k == 0 else shift_by(s, places - k, places) for k, s in zip(order, sums)]
    return place_rows([[taken[b][1] for b in g] for g in groups], plan, returned, blocks, rows)


def general_path(capacity, pieces, embeddings, row_count, fetch_list, left, right, pairs):
    places = lax.axis_size("blk")
    me = lax.axis_index("blk")
    sub = lax.axis_index("sub")
    blocks, rows, width = embeddings.shape
    total = places * capacity
    local_ids = jnp.arange(blocks, dtype=jnp.int32)
    slot_ids = jnp.arange(total, dtype=jnp.int32)
    owned = me * blocks + local_ids
    here = fetch_list[:, :, None] == owned[None, None, :]
    scorer = jnp.sum(jnp.where(here, jnp.arange(places, dtype=jnp.int32)[:, None, None], 0), axis=(0, 1))
    same = scorer[:, None] == scorer[None, :]
    rank = jnp.sum(same & (local_ids[None, :] < local_ids[:, None]), axis=1)
    send_slot = scorer * capacity + rank
    placing = send_slot[:, None] == slot_ids[None, :]
    source = jnp.sum(jnp.where(placing, local_ids[:, None], 0), axis=0)
    exchange = lambda x: lax.all_to_all(x, "blk", split_axis=0, concat_axis=0, tiled=True)
    mark = jax.vmap(lambda block, count: block.at[:, :LANES].set(marked(block[:, :LANES], sub, count)))
    incoming = exchange(jnp.take(mark(embeddings, row_count), source, axis=0))
    wanted = lax.dynamic_index_in_dim(fetch_list, me, 0, keepdims=False)
    owner, local = wanted // blocks, wanted % blocks
    together = owner[:, None] == owner[None, :]
    recv_rank = jnp.sum(together & (local[None, :] < local[:, None]), axis=1)
    recv_slot = owner * capacity + recv_rank
    live = jnp.arange(left.shape[1], dtype=jnp.int32) < pairs[0]
    one = jnp.int32(1)
    hot = lambda at: jnp.where(live[:, None], (at[:, None] == jnp.arange(blocks * blocks)).astype(jnp.int32), 0)
    listed = jnp.max(hot(left[0] * blocks + right[0]) | hot(right[0] * blocks + left[0]), axis=0)
    bits = jnp.sum(listed * lax.shift_left(one, jnp.arange(blocks * blocks, dtype=jnp.int32)))
    held = {}
    for b in range(blocks):
        block = lax.dynamic_index_in_dim(incoming, recv_slot[b], 0, keepdims=False)
        for q in range(pieces):
            held[b, q] = (swap_with(block, q, pieces) if q else block), 0, rows
    runs = range(blocks * pieces // 2)
    meta = local_ids, range(blocks), bits[None].astype(jnp.int32), [list(range(blocks))], []
    (dense,) = score(pieces, held, range(blocks), runs, [(0, blocks, 0, len(runs))], meta, name="score_all")
    back = (recv_slot[None, :] == slot_ids[:, None]).astype(jnp.float32)
    returned = exchange(jnp.sum(back[:, :, None] * dense[None, :, :], axis=1))
    return jnp.take(returned, send_slot, axis=0)


def body(embeddings, row_count, fetch_list, pair_left, pair_right, pair_count):
    places = lax.axis_size("blk")
    pieces = lax.axis_size("sub")
    blocks = embeddings.shape[0]
    capacity = (blocks + places - 1) // places
    given = (embeddings, row_count, fetch_list, pair_left, pair_right, pair_count)
    general = functools.partial(general_path, capacity, pieces)
    patterns = block_patterns(places, capacity, blocks)
    if not patterns or pieces != 4:
        return general(*given)
    me = lax.axis_index("blk").astype(jnp.int32)[None]
    sub = lax.axis_index("sub").astype(jnp.int32)[None]
    plan, bits, own, slots = make_plan(patterns, places, capacity, me, sub, *given)
    rows = embeddings.shape[1]
    branches = [
        lambda plan, bits, own, slots, given, counts=counts: pattern_path(counts, capacity, pieces, rows, plan, bits, own, slots)
        for counts in patterns
    ] + [lambda plan, bits, own, slots, given: general(*given)]
    return lax.switch(plan[0], branches, plan, bits, own, slots, given)


def solution(mesh):
    in_specs = (
        P(("parts", "blk"), "sub", None),
        P(("parts", "blk")),
        P("parts", None),
        P(("parts", "blk"), None),
        P(("parts", "blk"), None),
        P(("parts", "blk")),
    )
    out_specs = P(("parts", "blk"), "sub")
    return jax.shard_map(body, mesh=mesh, in_specs=in_specs, out_specs=out_specs, check_vma=False)
```

```python
import functools
import itertools
import math

import jax
import jax.numpy as jnp
from jax import lax
from jax.experimental import pallas as pl
from jax.experimental.pallas import tpu as pltpu
from jax.sharding import PartitionSpec as P

kernel_scale = 24.0
norm_eps = 1e-06
LANES = 128
FLOPS = 4
UNUSED = 2.0 ** 60
UNUSED_SQUARES = 2.0 ** 100
SCALE_IN_USE = 2.0 ** -30
VMEM_LIMIT = 24 * 1024 * 1024
ANY = pl.BlockSpec(memory_space=pl.ANY)
SMEM = pl.BlockSpec(memory_space=pltpu.SMEM)
VMEM = pl.BlockSpec(memory_space=pltpu.VMEM)


def block_patterns(places, capacity, blocks):
    if capacity < 2 or places > 4:
        return []
    cost = lambda counts: sum(c * min(k, places - k) for k, c in enumerate(counts))
    best = {}
    for counts in itertools.product(range(capacity + 1), repeat=places):
        if sum(counts) != blocks:
            continue
        turns = [counts[t:] + counts[:t] for t in range(places)]
        pick = min(turns, key=lambda c: (-c[0], cost(c), c))
        best[min(turns)] = pick
    return sorted(best.values(), key=cost)


def owner_of(block, blocks, places):
    return sum((block >= i * blocks).astype(jnp.int32) for i in range(1, places))


def unary(counts):
    return sum(((1 << c) - 1) << (2 * r) for r, c in enumerate(counts))


def marked(first_lanes, sub, count):
    rows, lanes = first_lanes.shape
    row = lax.broadcasted_iota(jnp.int32, (rows, lanes), 0) + sub * rows
    lane = lax.broadcasted_iota(jnp.int32, (rows, lanes), 1)
    return jnp.where((row >= count) & (lane == 0), UNUSED, first_lanes.astype(jnp.float32)).astype(first_lanes.dtype)


def plan_kernel(patterns, places, capacity, me_ref, sub_ref, fetch_ref, count_ref, left_ref, right_ref, pairs_ref,
                emb_ref, plan_ref, bits_ref, *rest):
    slots, sems = rest[:-1], rest[-1]
    blocks = count_ref.shape[0]
    rows = emb_ref.shape[1]
    views = [slots[0].at[pl.ds(j * rows, rows)] for j in range(capacity)] + list(slots[1:])
    me = me_ref[0]
    used = jnp.int32(0)
    for s in range(places):
        seen = jnp.int32(0)
        for p in range(blocks):
            owner = owner_of(fetch_ref[s, p], blocks, places)
            turned = owner - s
            bit = lax.shift_left(jnp.int32(1), 2 * jnp.where(turned < 0, turned + places, turned))
            seen = seen | bit | ((seen & bit) << 1)
        used = used | seen
    choice = jnp.int32(len(patterns))
    shift = jnp.int32(0)
    for m in reversed(range(len(patterns))):
        for t in range(places):
            allowed = unary([patterns[m][(t - r) % places] for r in range(places)])
            fits = (used & ~allowed) == 0
            choice = jnp.where(fits, m, choice)
            shift = jnp.where(fits, t, shift)
    plan_ref[0] = choice
    plan_ref[plan_ref.shape[0] - 1] = me
    plan_ref[1] = shift
    mine = lax.rem(me + places - shift, places)
    total = places * capacity
    copies = []
    for k in range(places):
        owner = lax.rem(me + places - k, places)
        target = lax.rem(me + k + places - shift, places)
        place, seen = [jnp.int32(0)] * capacity, jnp.int32(0)
        send, spot, sent = [jnp.int32(0)] * capacity, [jnp.int32(0)] * capacity, jnp.int32(0)
        for p in range(blocks):
            listed = fetch_ref[mine, p]
            hit = owner_of(listed, blocks, places) == owner
            outward = fetch_ref[target, p]
            goes = owner_of(outward, blocks, places) == me
            for j in range(capacity):
                place[j] = jnp.where(hit & (seen == j), p, place[j])
                send[j] = jnp.where(goes & (sent == j), outward - me * blocks, send[j])
                spot[j] = jnp.where(goes & (sent == j), p, spot[j])
            seen = seen + hit.astype(jnp.int32)
            sent = sent + goes.astype(jnp.int32)
        for j in range(capacity):
            at = k * capacity + j
            copy = pltpu.make_async_copy(emb_ref.at[send[j]], views[at], sems.at[at])
            pl.when(sent > j)(copy.start)
            copies.append((sent > j, copy))
            plan_ref[2 + at] = send[j]
            plan_ref[2 + total + at] = place[j]
            plan_ref[2 + 2 * total + at] = spot[j]
    bits = jnp.int32(0)
    for p in range(left_ref.shape[1]):
        a, b = left_ref[0, p], right_ref[0, p]
        both = lax.shift_left(jnp.int32(1), a * blocks + b) | lax.shift_left(jnp.int32(1), b * blocks + a)
        bits = bits | jnp.where(p < pairs_ref[0], both, 0)
    bits_ref[0] = bits
    for at, (filled, copy) in enumerate(copies):
        pl.when(filled)(copy.wait)
        views[at][:, :LANES] = marked(views[at][:, :LANES], sub_ref[0], count_ref[plan_ref[2 + at]])


def make_plan(patterns, places, capacity, me, sub, embeddings, row_count, fetch_list, left, right, pairs):
    blocks, rows, width = embeddings.shape
    total = places * capacity
    slot = jax.ShapeDtypeStruct((rows, width), embeddings.dtype)
    own = jax.ShapeDtypeStruct((capacity * rows, width), embeddings.dtype)
    others = total - capacity
    out = pl.pallas_call(
        functools.partial(plan_kernel, patterns, places, capacity),
        out_shape=[jax.ShapeDtypeStruct((3 + 3 * total,), jnp.int32),
                   jax.ShapeDtypeStruct((1,), jnp.int32), own] + [slot] * others,
        in_specs=[SMEM] * 7 + [ANY],
        out_specs=[SMEM, SMEM] + [VMEM] * (1 + others),
        scratch_shapes=[pltpu.SemaphoreType.DMA((total,))],
        name="plan_and_gather",
    )(me, sub, fetch_list, row_count, left, right, pairs, embeddings)
    return out[0], out[1], out[2], out[3:]


def pairs_of(per, runs, steps):
    return [(a, b) for lo, hi, start, end in steps
            for b in sorted({runs[run] // per for run in range(start, end)}) for a in range(lo, hi)]


def score_kernel(rows, width, pieces, wheres, owned, runs, steps, places, *refs):
    refs = list(refs)
    arrays = [refs.pop(0) for _ in range(1 + max(i for i, _ in wheres))]
    spots_in = [arrays[i].at[pl.ds(n * rows, rows)] for i, n in wheres]
    left_in, right_in = spots_in[:len(owned)], spots_in[len(owned):]
    finish = passed = None
    if places is not None:
        finish = [refs.pop(0) for _ in range(2 + places[0])]
        if not owned:
            passed = refs.pop(0), refs.pop(0)
    hand_on = places is None
    out_refs = [refs.pop(0) for _ in (places[2] if places and places[2] else range(1 + 2 * hand_on))]
    if hand_on:
        right, gram, left_sems, right_sems = refs[:4]
        left, left_scale = out_refs[1:]
    elif passed is None:
        left, right, left_scale, gram, left_sems, right_sems = refs[:6]
    else:
        right, gram, right_sems = refs[:3]
        left, left_scale = passed
    sums = refs[-1] if places else out_refs[0]
    per = pieces // 2
    copies = []
    for i, a in enumerate(owned):
        copies.append(pltpu.make_async_copy(left_in[i], left.at[pl.ds(i * rows, rows)], left_sems.at[i]))
    for i in range(2 * len(runs)):
        copies.append(pltpu.make_async_copy(right_in[i], right.at[pl.ds(i * rows, rows)], right_sems.at[i]))
    for copy in copies:
        copy.start()
    eye = lax.broadcasted_iota(jnp.int32, (rows, rows), 0) == lax.broadcasted_iota(jnp.int32, (rows, rows), 1)

    def squares(block):
        wide = block.astype(jnp.float32)
        return jnp.sum(wide * wide, axis=1, keepdims=True)

    def lanes(col):
        return jnp.sum(jnp.where(eye, col, 0.0), axis=0, keepdims=True)

    for i in range(len(owned)):
        copies[i].wait()

    @pl.loop(0, len(owned))
    def _(i):
        here = pl.ds(pl.multiple_of(i * rows, rows), rows)
        inv = lax.rsqrt(squares(left[here, :]) * (1.0 / width) + norm_eps)
        left_scale[here, :] = jnp.broadcast_to(inv * (kernel_scale / width * math.log2(math.e)), (rows, rows))

    arrived = base = 0
    for lo, hi, start, end in steps:
        fresh = end > arrived
        first_block = runs[start] // per

        @pl.loop(start, end)
        def _(run):
            if fresh:
                for h in range(2):
                    pltpu.make_async_copy(
                        right_in[0], right.at[pl.ds((2 * run + h) * rows, rows)], right_sems.at[2 * run + h]).wait()
            flat = runs[0] + run
            b = lax.div(flat, per)
            q = 2 * lax.rem(flat, per)
            scale_row, valid = [], []
            for h in range(2):
                here = pl.ds(pl.multiple_of((2 * run + h) * rows, rows), rows)
                total = lanes(squares(right[here, :]))
                scale_row.append(lax.rsqrt(total * (1.0 / width) + norm_eps))
                valid.append((total < UNUSED_SQUARES).astype(jnp.float32))
            both = right[pl.ds(pl.multiple_of(2 * run * rows, rows), 2 * rows), :]
            gram[:(hi - lo) * rows, :] = lax.dot_general(
                left[lo * rows:hi * rows, :], both, (((1,), (1,)), ((), ())), preferred_element_type=jnp.float32)
            for a in range(lo, hi):
                there = slice((a - lo) * rows, (a - lo + 1) * rows)
                scale = left_scale[a * rows:(a + 1) * rows, :]
                same = eye & ((b == a) & (q == 0))
                near = jnp.exp2(gram[there, :rows] * scale * scale_row[0]) * valid[0]
                far = jnp.exp2(gram[there, rows:] * scale * scale_row[1]) * valid[1]
                tile = jnp.where(same, 0.0, near) + far
                pair = base + (b - first_block) * (hi - lo) + a - lo
                if end - start > 1:
                    tile = tile + jnp.where(q == 0, 0.0, sums[pair])
                sums[pair] = tile

        arrived = max(arrived, end)
        base += (runs[end - 1] // per + 1 - first_block) * (hi - lo)
    if places is None:
        return
    count, spots, groups, listed = places
    plan_ref, bits_ref = finish[:2]
    bits = bits_ref[0]
    spot = [plan_ref[at] for at in spots]
    blocks = len(spots)
    if groups is None:
        for a in range(blocks):
            in_use = left_scale[a * rows:(a + 1) * rows, :1] > SCALE_IN_USE
            by_block = {}
            for source, at, b in listed[a]:
                part = (sums if source < 0 else finish[2 + source])[at]
                by_block[b] = by_block[b] + part if b in by_block else part
            for b, part in by_block.items():
                total = jnp.where(in_use, jnp.sum(part, axis=1, keepdims=True), 0.0)
                out_refs[0][pl.ds(a * blocks + spot[b], 1), :] = lanes(total)
        lane = lax.broadcasted_iota(jnp.int32, (1, rows), 1)
        flags = sum(jnp.where(lane == i, (bits >> i) & 1, 0) for i in range(blocks * blocks))
        out_refs[0][blocks * blocks:blocks * blocks + 1, :] = flags.astype(jnp.float32)
        return
    for ref, group in zip(out_refs, groups):
        for n, a in enumerate(group):
            total = jnp.zeros((rows, rows), jnp.float32)
            for source, at, right_block in listed[a]:
                paired = (bits >> (spot[a] * blocks + spot[right_block])) & 1
                total = total + (sums if source < 0 else finish[2 + source])[at] * paired.astype(jnp.float32)
            total = jnp.sum(total, axis=1, keepdims=True)
            total = jnp.where(left_scale[a * rows:(a + 1) * rows, :1] > SCALE_IN_USE, total, 0.0)
            ref[n:n + 1, :] = jnp.log1p(lanes(total) / (pieces * rows))


def score(pieces, held, owned, runs, steps, meta=None, name="score"):
    array, _, rows = held[0, 0]
    width = array.shape[1]
    per = pieces // 2
    rights = [held[run // per, 2 * (run % per) + h] for run in runs for h in range(2)]
    arrays, wheres = [], []
    for array, n, _ in [held[a, 0] for a in owned] + rights:
        known = [i for i, other in enumerate(arrays) if other is array]
        if not known:
            arrays.append(array)
        wheres.append((known[0] if known else len(arrays) - 1, n))
    tall = max(hi - lo for lo, hi, _, _ in steps) * rows
    pairs = pairs_of(per, runs, steps)
    sums = jax.ShapeDtypeStruct((len(pairs), rows, rows), jnp.float32)
    tall_left = len(owned) * rows
    lefts = [(tall_left, width), jnp.bfloat16], [(tall_left, rows), jnp.float32]
    places, extra, extra_specs, out_shape, scratch = None, [], [], [sums] + [jax.ShapeDtypeStruct(*x) for x in lefts], []
    if meta is not None:
        plan, spots, bits, groups, earlier, passed = meta
        listed = [[] for _ in spots]
        for source, (_, known) in enumerate(earlier + [(None, pairs)]):
            for at, (a, b) in enumerate(known):
                listed[a].append((source if source < len(earlier) else -1, at, b))
        places = len(earlier), spots, groups, listed
        extra = [plan, bits] + [array for array, _ in earlier] + list(passed)
        extra_specs = [SMEM, SMEM] + [VMEM] * (len(earlier) + len(passed))
        count = -(-(len(spots) ** 2 + 1) // 8) * 8
        out_shape = [jax.ShapeDtypeStruct((len(g), rows), jnp.float32) for g in groups or [range(count)]]
        scratch = [pltpu.VMEM(sums.shape, jnp.float32)]
    keeps = meta is not None and owned
    flops = sum(4 * (hi - lo) * (end - start) * rows * rows * width for lo, hi, start, end in steps)
    moved = (len(owned) + len(rights)) * rows * width * 2
    result = pl.pallas_call(
        functools.partial(score_kernel, rows, width, pieces, wheres, owned, runs, steps, places),
        out_shape=out_shape,
        in_specs=[ANY] * len(arrays) + extra_specs,
        out_specs=[VMEM] * len(out_shape),
        scratch_shapes=([pltpu.VMEM(*lefts[0])] if keeps else []) + [
            pltpu.VMEM((len(rights) * rows, width), jnp.bfloat16)] + ([pltpu.VMEM(*lefts[1])] if keeps else []) + [
            pltpu.VMEM((tall, 2 * rows), jnp.float32)] + (
            [pltpu.SemaphoreType.DMA((len(owned),))] if owned else []) + [
            pltpu.SemaphoreType.DMA((len(rights),)),
        ] + scratch,
        compiler_params=pltpu.CompilerParams(vmem_limit_bytes=VMEM_LIMIT),
        cost_estimate=pl.CostEstimate(flops=0, bytes_accessed=0, transcendentals=0),
        name=name,
    )(*arrays, *extra)
    return (result[0], pairs, result[1:]) if meta is None else result


def place_kernel(taken, capacity, pieces, plan_ref, *refs):
    refs, out_ref, held = refs[:-2], refs[-2], refs[-1]
    places = len(refs)
    blocks, rows = out_ref.shape
    total = places * capacity
    me = plan_ref[plan_ref.shape[0] - 1]
    for q, ref in enumerate(refs):
        held[q] = ref[...]
    lane = lax.broadcasted_iota(jnp.int32, (blocks, rows), 1)
    spot = lax.broadcasted_iota(jnp.int32, (blocks, rows), 0)
    for n, (k, at) in enumerate(taken):
        scorer = lax.rem(me + k, places)
        group = lax.rem(scorer + places - plan_ref[1], places)
        flags = held[me ^ group, blocks * blocks:blocks * blocks + 1, :]
        first = plan_ref[2 + 2 * total + at] * blocks
        paired = jnp.sum(jnp.where(lane == spot + first, flags, 0.0), axis=1, keepdims=True)
        sums = held[me ^ scorer, n * blocks:(n + 1) * blocks, :]
        sums = jnp.sum(jnp.where(paired > 0.0, sums, 0.0), axis=0, keepdims=True)
        out_ref[pl.ds(plan_ref[2 + at], 1), :] = jnp.log1p(sums / (pieces * rows))


def place_rows(taken, capacity, pieces, plan, returned, blocks, rows):
    return pl.pallas_call(
        functools.partial(place_kernel, taken, capacity, pieces),
        out_shape=jax.ShapeDtypeStruct((blocks, rows), jnp.float32),
        in_specs=[SMEM] + [VMEM] * len(returned),
        out_specs=VMEM,
        scratch_shapes=[pltpu.VMEM((len(returned),) + returned[0].shape, jnp.float32)],
        name="place_rows",
    )(plan, *returned)


def shift_by(array, k, places):
    return lax.ppermute(array, "blk", [(i, (i + k) % places) for i in range(places)])


def swap_with(array, q, pieces):
    return lax.ppermute(array, "sub", [(i, i ^ q) for i in range(pieces)])


def after(array, *others):
    return lax.optimization_barrier((array,) + others)[0]


def pattern_path(counts, capacity, pieces, rows, plan, bits, own, slots):
    places = len(counts)
    nearest = sorted((k for k in range(1, places) if counts[k]), key=lambda k: min(k, places - k))
    sets = [[(0, j) for j in range(counts[0])], [(nearest[0], 0)], [(nearest[1], 0)],
            [(k, 0) for k in nearest[2:]] + [(k, 1) for k in nearest if counts[k] > 1]]
    taken = [(k, k * capacity + j) for group in sets for k, j in group]
    blocks = len(taken)
    per = pieces // 2
    moved = []
    for k, at in taken:
        if k:
            sent = slots[at - capacity]
            if len(moved) == 2:
                sent = after(sent, moved[0])
            moved.append(shift_by(sent, k, places))
    arrived = [own if len(sets[0]) == capacity else own[:rows], moved[0], moved[1],
               moved[2] if len(moved) == 3 else jnp.concatenate(moved[2:], axis=0)]
    held = {}
    first = [0, len(sets[0]), len(sets[0]) + 1, len(sets[0]) + 2, blocks]
    ready, end = first[1], first[3]
    acrosses = []
    for g, array in enumerate(arrived):
        across = swap_with(array, 2, pieces)
        acrosses.append(across)
        beside = swap_with(array, 1, pieces)
        for n, b in enumerate(range(first[g], first[g + 1])):
            held[b, 0], held[b, 1], held[b, 2] = (array, n, rows), (beside, n, rows), (across, n, rows)
        if g == 3:
            runs = range(end * per + (per - 1) * (blocks - end == 1))
            most = score(pieces, held, range(blocks), runs, [(0, blocks, 0, len(runs))], name="score_most")
            across = after(across, most[0])
        corner = swap_with(across, 1, pieces)
        for n, b in enumerate(range(first[g], first[g + 1])):
            held[b, 3] = (corner, n, rows)
    (dense,) = score(pieces, held, range(0), range(len(runs), blocks * per), [(0, blocks, 0, blocks * per - len(runs))],
                     (plan, [2 + places * capacity + at for _, at in taken], bits, None, [most[:2]], most[2]),
                     name="score_late")
    returned = [dense] + [lax.ppermute(dense, "blk", [(i, i ^ q) for i in range(places)]) for q in range(1, places)]
    return place_rows(taken, capacity, pieces, plan, returned, blocks, rows)


def general_path(capacity, pieces, embeddings, row_count, fetch_list, left, right, pairs):
    places = lax.axis_size("blk")
    me = lax.axis_index("blk")
    sub = lax.axis_index("sub")
    blocks, rows, width = embeddings.shape
    total = places * capacity
    local_ids = jnp.arange(blocks, dtype=jnp.int32)
    slot_ids = jnp.arange(total, dtype=jnp.int32)
    owned = me * blocks + local_ids
    here = fetch_list[:, :, None] == owned[None, None, :]
    scorer = jnp.sum(jnp.where(here, jnp.arange(places, dtype=jnp.int32)[:, None, None], 0), axis=(0, 1))
    same = scorer[:, None] == scorer[None, :]
    rank = jnp.sum(same & (local_ids[None, :] < local_ids[:, None]), axis=1)
    send_slot = scorer * capacity + rank
    placing = send_slot[:, None] == slot_ids[None, :]
    source = jnp.sum(jnp.where(placing, local_ids[:, None], 0), axis=0)
    exchange = lambda x: lax.all_to_all(x, "blk", split_axis=0, concat_axis=0, tiled=True)
    mark = jax.vmap(lambda block, count: block.at[:, :LANES].set(marked(block[:, :LANES], sub, count)))
    incoming = exchange(jnp.take(mark(embeddings, row_count), source, axis=0))
    wanted = lax.dynamic_index_in_dim(fetch_list, me, 0, keepdims=False)
    owner, local = wanted // blocks, wanted % blocks
    together = owner[:, None] == owner[None, :]
    recv_rank = jnp.sum(together & (local[None, :] < local[:, None]), axis=1)
    recv_slot = owner * capacity + recv_rank
    live = jnp.arange(left.shape[1], dtype=jnp.int32) < pairs[0]
    one = jnp.int32(1)
    hot = lambda at: jnp.where(live[:, None], (at[:, None] == jnp.arange(blocks * blocks)).astype(jnp.int32), 0)
    listed = jnp.max(hot(left[0] * blocks + right[0]) | hot(right[0] * blocks + left[0]), axis=0)
    bits = jnp.sum(listed * lax.shift_left(one, jnp.arange(blocks * blocks, dtype=jnp.int32)))
    held = {}
    for b in range(blocks):
        block = lax.dynamic_index_in_dim(incoming, recv_slot[b], 0, keepdims=False)
        for q in range(pieces):
            held[b, q] = (swap_with(block, q, pieces) if q else block), 0, rows
    runs = range(blocks * pieces // 2)
    meta = local_ids, range(blocks), bits[None].astype(jnp.int32), [list(range(blocks))], [], []
    (dense,) = score(pieces, held, range(blocks), runs, [(0, blocks, 0, len(runs))], meta, name="score_all")
    back = (recv_slot[None, :] == slot_ids[:, None]).astype(jnp.float32)
    returned = exchange(jnp.sum(back[:, :, None] * dense[None, :, :], axis=1))
    return jnp.take(returned, send_slot, axis=0)


def body(embeddings, row_count, fetch_list, pair_left, pair_right, pair_count):
    places = lax.axis_size("blk")
    pieces = lax.axis_size("sub")
    blocks = embeddings.shape[0]
    capacity = (blocks + places - 1) // places
    given = (embeddings, row_count, fetch_list, pair_left, pair_right, pair_count)
    general = functools.partial(general_path, capacity, pieces)
    patterns = block_patterns(places, capacity, blocks)
    if not patterns or pieces != 4:
        return general(*given)
    me = lax.axis_index("blk").astype(jnp.int32)[None]
    sub = lax.axis_index("sub").astype(jnp.int32)[None]
    plan, bits, own, slots = make_plan(patterns, places, capacity, me, sub, *given)
    rows = embeddings.shape[1]
    branches = [
        lambda plan, bits, own, slots, given, counts=counts: pattern_path(counts, capacity, pieces, rows, plan, bits, own, slots)
        for counts in patterns
    ] + [lambda plan, bits, own, slots, given: general(*given)]
    return lax.switch(plan[0], branches, plan, bits, own, slots, given)


def solution(mesh):
    in_specs = (
        P(("parts", "blk"), "sub", None),
        P(("parts", "blk")),
        P("parts", None),
        P(("parts", "blk"), None),
        P(("parts", "blk"), None),
        P(("parts", "blk")),
    )
    out_specs = P(("parts", "blk"), "sub")
    return jax.shard_map(body, mesh=mesh, in_specs=in_specs, out_specs=out_specs, check_vma=False)
```

```python
import functools
import itertools
import math

import jax
import jax.numpy as jnp
from jax import lax
from jax.experimental import pallas as pl
from jax.experimental.pallas import tpu as pltpu
from jax.sharding import PartitionSpec as P

kernel_scale = 24.0
norm_eps = 1e-06
LANES = 128
FLOPS = 4
UNUSED = 2.0 ** 60
UNUSED_SQUARES = 2.0 ** 100
SCALE_IN_USE = 2.0 ** -30
VMEM_LIMIT = 24 * 1024 * 1024
ANY = pl.BlockSpec(memory_space=pl.ANY)
SMEM = pl.BlockSpec(memory_space=pltpu.SMEM)
VMEM = pl.BlockSpec(memory_space=pltpu.VMEM)


def block_patterns(places, capacity, blocks):
    if capacity < 2 or places > 4:
        return []
    cost = lambda counts: sum(c * min(k, places - k) for k, c in enumerate(counts))
    best = {}
    for counts in itertools.product(range(capacity + 1), repeat=places):
        if sum(counts) != blocks:
            continue
        turns = [counts[t:] + counts[:t] for t in range(places)]
        pick = min(turns, key=lambda c: (-c[0], cost(c), c))
        best[min(turns)] = pick
    return sorted(best.values(), key=cost)


def owner_of(block, blocks, places):
    return sum((block >= i * blocks).astype(jnp.int32) for i in range(1, places))


def slots_of(counts, capacity):
    places = len(counts)
    nearest = sorted((k for k in range(1, places) if counts[k]), key=lambda k: min(k, places - k))
    order = [(0, j) for j in range(counts[0])] + [(k, 0) for k in nearest] + [(k, 1) for k in nearest if counts[k] > 1]
    return [(k, k * capacity + j) for k, j in order]


def unary(counts):
    return sum(((1 << c) - 1) << (2 * r) for r, c in enumerate(counts))


def marked(first_lanes, sub, count):
    rows, lanes = first_lanes.shape
    row = lax.broadcasted_iota(jnp.int32, (rows, lanes), 0) + sub * rows
    lane = lax.broadcasted_iota(jnp.int32, (rows, lanes), 1)
    return jnp.where((row >= count) & (lane == 0), UNUSED, first_lanes.astype(jnp.float32)).astype(first_lanes.dtype)


def plan_kernel(patterns, places, capacity, me_ref, sub_ref, fetch_ref, count_ref, left_ref, right_ref, pairs_ref,
                emb_ref, plan_ref, bits_ref, *rest):
    slots, sems = rest[:-1], rest[-1]
    blocks = count_ref.shape[0]
    rows = emb_ref.shape[1]
    views = [slots[0].at[pl.ds(j * rows, rows)] for j in range(capacity)] + list(slots[1:])
    me = me_ref[0]
    used = jnp.int32(0)
    for s in range(places):
        seen = jnp.int32(0)
        for p in range(blocks):
            owner = owner_of(fetch_ref[s, p], blocks, places)
            turned = owner - s
            bit = lax.shift_left(jnp.int32(1), 2 * jnp.where(turned < 0, turned + places, turned))
            seen = seen | bit | ((seen & bit) << 1)
        used = used | seen
    choice = jnp.int32(len(patterns))
    shift = jnp.int32(0)
    for m in reversed(range(len(patterns))):
        for t in range(places):
            allowed = unary([patterns[m][(t - r) % places] for r in range(places)])
            fits = (used & ~allowed) == 0
            choice = jnp.where(fits, m, choice)
            shift = jnp.where(fits, t, shift)
    plan_ref[0] = choice
    plan_ref[plan_ref.shape[0] - 1] = me
    plan_ref[1] = shift
    mine = lax.rem(me + places - shift, places)
    total = places * capacity
    copies = []
    for k in range(places):
        owner = lax.rem(me + places - k, places)
        target = lax.rem(me + k + places - shift, places)
        place, seen = [jnp.int32(0)] * capacity, jnp.int32(0)
        send, spot, sent = [jnp.int32(0)] * capacity, [jnp.int32(0)] * capacity, jnp.int32(0)
        for p in range(blocks):
            listed = fetch_ref[mine, p]
            hit = owner_of(listed, blocks, places) == owner
            outward = fetch_ref[target, p]
            goes = owner_of(outward, blocks, places) == me
            for j in range(capacity):
                place[j] = jnp.where(hit & (seen == j), p, place[j])
                send[j] = jnp.where(goes & (sent == j), outward - me * blocks, send[j])
                spot[j] = jnp.where(goes & (sent == j), p, spot[j])
            seen = seen + hit.astype(jnp.int32)
            sent = sent + goes.astype(jnp.int32)
        for j in range(capacity):
            at = k * capacity + j
            copy = pltpu.make_async_copy(emb_ref.at[send[j]], views[at], sems.at[at])
            pl.when(sent > j)(copy.start)
            copies.append((sent > j, copy))
            plan_ref[2 + at] = send[j]
            plan_ref[2 + total + at] = place[j]
            plan_ref[2 + 2 * total + at] = spot[j]
    bits = jnp.int32(0)
    for p in range(left_ref.shape[1]):
        a, b = left_ref[0, p], right_ref[0, p]
        both = lax.shift_left(jnp.int32(1), a * blocks + b) | lax.shift_left(jnp.int32(1), b * blocks + a)
        bits = bits | jnp.where(p < pairs_ref[0], both, 0)
    bits_ref[0] = bits
    for at, (filled, copy) in enumerate(copies):
        pl.when(filled)(copy.wait)
        views[at][:, :LANES] = marked(views[at][:, :LANES], sub_ref[0], count_ref[plan_ref[2 + at]])


def make_plan(patterns, places, capacity, me, sub, embeddings, row_count, fetch_list, left, right, pairs):
    blocks, rows, width = embeddings.shape
    total = places * capacity
    slot = jax.ShapeDtypeStruct((rows, width), embeddings.dtype)
    own = jax.ShapeDtypeStruct((capacity * rows, width), embeddings.dtype)
    others = total - capacity
    out = pl.pallas_call(
        functools.partial(plan_kernel, patterns, places, capacity),
        out_shape=[jax.ShapeDtypeStruct((3 + 3 * total,), jnp.int32),
                   jax.ShapeDtypeStruct((1,), jnp.int32), own] + [slot] * others,
        in_specs=[SMEM] * 7 + [ANY],
        out_specs=[SMEM, SMEM] + [VMEM] * (1 + others),
        scratch_shapes=[pltpu.SemaphoreType.DMA((total,))],
        name="plan_and_gather",
    )(me, sub, fetch_list, row_count, left, right, pairs, embeddings)
    return out[0], out[1], out[2], out[3:]


def pairs_of(per, runs, steps):
    return [(a, b) for lo, hi, start, end in steps
            for b in sorted({runs[run] // per for run in range(start, end)}) for a in range(lo, hi)]


def score_kernel(rows, width, pieces, wheres, owned, runs, steps, places, *refs):
    refs = list(refs)
    arrays = [refs.pop(0) for _ in range(1 + max(i for i, _ in wheres))]
    spots_in = [arrays[i].at[pl.ds(n * rows, rows)] for i, n in wheres]
    right_in = spots_in
    finish = passed = None
    if places is not None:
        finish = [refs.pop(0) for _ in range(2 + places[0])]
        if not owned:
            passed = refs.pop(0), refs.pop(0)
    hand_on = places is None
    out_refs = [refs.pop(0) for _ in (places[2] if places and places[2] else range(1 + 2 * hand_on))]
    if hand_on:
        right, gram, right_sems = refs[:3]
        left, left_scale = out_refs[1:]
    elif passed is None:
        left, right, left_scale, gram, right_sems = refs[:5]
    else:
        right, gram, right_sems = refs[:3]
        left, left_scale = passed
    sums = refs[-1] if places else out_refs[0]
    per = pieces // 2
    copies = []
    for i in range(2 * len(runs)):
        copies.append(pltpu.make_async_copy(right_in[i], right.at[pl.ds(i * rows, rows)], right_sems.at[i]))
    for copy in copies:
        copy.start()
    eye = lax.broadcasted_iota(jnp.int32, (rows, rows), 0) == lax.broadcasted_iota(jnp.int32, (rows, rows), 1)

    def squares(block):
        wide = block.astype(jnp.float32)
        return jnp.sum(wide * wide, axis=1, keepdims=True)

    def lanes(col):
        return jnp.sum(jnp.where(eye, col, 0.0), axis=0, keepdims=True)

    @pl.loop(0, len(owned))
    def _(i):
        here = pl.ds(pl.multiple_of(i * rows, rows), rows)
        there = pl.ds(pl.multiple_of(i * pieces * rows, rows), rows)
        pltpu.make_async_copy(right_in[0], right.at[there], right_sems.at[i * pieces]).wait()
        left[here, :] = right[there, :]
        inv = lax.rsqrt(squares(left[here, :]) * (1.0 / width) + norm_eps)
        left_scale[here, :] = jnp.broadcast_to(inv * (kernel_scale / width * math.log2(math.e)), (rows, rows))

    arrived = base = 0
    for lo, hi, start, end in steps:
        fresh = end > arrived
        first_block = runs[start] // per

        @pl.loop(start, end)
        def _(run):
            if fresh:
                for h in range(2):
                    copy = pltpu.make_async_copy(
                        right_in[0], right.at[pl.ds((2 * run + h) * rows, rows)], right_sems.at[2 * run + h])
                    if h == 0 and owned:
                        pl.when(lax.rem(runs[0] + run, per) != 0)(copy.wait)
                    else:
                        copy.wait()
            flat = runs[0] + run
            b = lax.div(flat, per)
            q = 2 * lax.rem(flat, per)
            scale_row, valid = [], []
            for h in range(2):
                here = pl.ds(pl.multiple_of((2 * run + h) * rows, rows), rows)
                total = lanes(squares(right[here, :]))
                scale_row.append(lax.rsqrt(total * (1.0 / width) + norm_eps))
                valid.append((total < UNUSED_SQUARES).astype(jnp.float32))
            both = right[pl.ds(pl.multiple_of(2 * run * rows, rows), 2 * rows), :]
            gram[:(hi - lo) * rows, :] = lax.dot_general(
                left[lo * rows:hi * rows, :], both, (((1,), (1,)), ((), ())), preferred_element_type=jnp.float32)
            for a in range(lo, hi):
                there = slice((a - lo) * rows, (a - lo + 1) * rows)
                scale = left_scale[a * rows:(a + 1) * rows, :]
                same = eye & ((b == a) & (q == 0))
                near = jnp.exp2(gram[there, :rows] * scale * scale_row[0]) * valid[0]
                far = jnp.exp2(gram[there, rows:] * scale * scale_row[1]) * valid[1]
                tile = jnp.where(same, 0.0, near) + far
                pair = base + (b - first_block) * (hi - lo) + a - lo
                if end - start > 1:
                    tile = tile + jnp.where(q == 0, 0.0, sums[pair])
                sums[pair] = tile

        arrived = max(arrived, end)
        base += (runs[end - 1] // per + 1 - first_block) * (hi - lo)
    if places is None:
        return
    count, spots, groups, listed = places
    plan_ref, bits_ref = finish[:2]
    bits = bits_ref[0]
    spot = [plan_ref[at] for at in spots]
    blocks = len(spots)
    if groups is None:
        for a in range(blocks):
            in_use = left_scale[a * rows:(a + 1) * rows, :] > SCALE_IN_USE
            by_block = {}
            for source, at, b in listed[a]:
                part = (sums if source < 0 else finish[2 + source])[at]
                by_block[b] = by_block[b] + part if b in by_block else part
            for b, part in by_block.items():
                total = jnp.sum(jnp.transpose(jnp.where(in_use, part, 0.0)), axis=0, keepdims=True)
                out_refs[0][pl.ds(a * blocks + spot[b], 1), :] = total
        lane = lax.broadcasted_iota(jnp.int32, (1, rows), 1)
        flags = sum(jnp.where(lane == i, (bits >> i) & 1, 0) for i in range(blocks * blocks))
        out_refs[0][blocks * blocks:blocks * blocks + 1, :] = flags.astype(jnp.float32)
        return
    for ref, group in zip(out_refs, groups):
        for n, a in enumerate(group):
            total = jnp.zeros((rows, rows), jnp.float32)
            for source, at, right_block in listed[a]:
                paired = (bits >> (spot[a] * blocks + spot[right_block])) & 1
                total = total + (sums if source < 0 else finish[2 + source])[at] * paired.astype(jnp.float32)
            total = jnp.sum(total, axis=1, keepdims=True)
            total = jnp.where(left_scale[a * rows:(a + 1) * rows, :1] > SCALE_IN_USE, total, 0.0)
            ref[n:n + 1, :] = jnp.log1p(lanes(total) / (pieces * rows))


def score(pieces, held, owned, runs, steps, meta=None, name="score"):
    array, _, rows = next(iter(held.values()))
    width = array.shape[1]
    per = pieces // 2
    rights = [held[run // per, 2 * (run % per) + h] for run in runs for h in range(2)]
    arrays, wheres = [], []
    for array, n, _ in rights:
        known = [i for i, other in enumerate(arrays) if other is array]
        if not known:
            arrays.append(array)
        wheres.append((known[0] if known else len(arrays) - 1, n))
    tall = max(hi - lo for lo, hi, _, _ in steps) * rows
    pairs = pairs_of(per, runs, steps)
    sums = jax.ShapeDtypeStruct((len(pairs), rows, rows), jnp.float32)
    tall_left = len(owned) * rows
    lefts = [(tall_left, width), jnp.bfloat16], [(tall_left, rows), jnp.float32]
    places, extra, extra_specs, out_shape, scratch = None, [], [], [sums] + [jax.ShapeDtypeStruct(*x) for x in lefts], []
    if meta is not None:
        plan, spots, bits, groups, earlier, passed = meta
        listed = [[] for _ in spots]
        for source, (_, known) in enumerate(earlier + [(None, pairs)]):
            for at, (a, b) in enumerate(known):
                listed[a].append((source if source < len(earlier) else -1, at, b))
        places = len(earlier), spots, groups, listed
        extra = [plan, bits] + [array for array, _ in earlier] + list(passed)
        extra_specs = [SMEM, SMEM] + [VMEM] * (len(earlier) + len(passed))
        count = -(-(len(spots) ** 2 + 1) // 8) * 8
        out_shape = [jax.ShapeDtypeStruct((len(g), rows), jnp.float32) for g in groups or [range(count)]]
        scratch = [pltpu.VMEM(sums.shape, jnp.float32)]
    keeps = meta is not None and owned
    flops = sum(4 * (hi - lo) * (end - start) * rows * rows * width for lo, hi, start, end in steps)
    moved = (len(owned) + len(rights)) * rows * width * 2
    result = pl.pallas_call(
        functools.partial(score_kernel, rows, width, pieces, wheres, owned, runs, steps, places),
        out_shape=out_shape,
        in_specs=[ANY] * len(arrays) + extra_specs,
        out_specs=[VMEM] * len(out_shape),
        scratch_shapes=([pltpu.VMEM(*lefts[0])] if keeps else []) + [
            pltpu.VMEM((len(rights) * rows, width), jnp.bfloat16)] + ([pltpu.VMEM(*lefts[1])] if keeps else []) + [
            pltpu.VMEM((tall, 2 * rows), jnp.float32),
            pltpu.SemaphoreType.DMA((len(rights),)),
        ] + scratch,
        compiler_params=pltpu.CompilerParams(vmem_limit_bytes=VMEM_LIMIT),
        cost_estimate=pl.CostEstimate(flops=0, bytes_accessed=0, transcendentals=0),
        name=name,
    )(*arrays, *extra)
    return (result[0], pairs, result[1:]) if meta is None else result


def place_kernel(taken, capacity, pieces, plan_ref, *refs):
    refs, out_ref, held = refs[:-2], refs[-2], refs[-1]
    places = len(refs)
    blocks, rows = out_ref.shape
    total = places * capacity
    me = plan_ref[plan_ref.shape[0] - 1]
    for q, ref in enumerate(refs):
        held[q] = ref[...]
    lane = lax.broadcasted_iota(jnp.int32, (blocks, rows), 1)
    spot = lax.broadcasted_iota(jnp.int32, (blocks, rows), 0)
    for n, (k, at) in enumerate(taken):
        scorer = lax.rem(me + k, places)
        group = lax.rem(scorer + places - plan_ref[1], places)
        flags = held[me ^ group, blocks * blocks:blocks * blocks + 1, :]
        first = plan_ref[2 + 2 * total + at] * blocks
        paired = jnp.sum(jnp.where(lane == spot + first, flags, 0.0), axis=1, keepdims=True)
        sums = held[me ^ scorer, n * blocks:(n + 1) * blocks, :]
        sums = jnp.sum(jnp.where(paired > 0.0, sums, 0.0), axis=0, keepdims=True)
        out_ref[pl.ds(plan_ref[2 + at], 1), :] = jnp.log1p(sums / (pieces * rows))


def place_rows(taken, capacity, pieces, plan, returned, blocks, rows):
    return pl.pallas_call(
        functools.partial(place_kernel, taken, capacity, pieces),
        out_shape=jax.ShapeDtypeStruct((blocks, rows), jnp.float32),
        in_specs=[SMEM] + [VMEM] * len(returned),
        out_specs=VMEM,
        scratch_shapes=[pltpu.VMEM((len(returned),) + returned[0].shape, jnp.float32)],
        name="place_rows",
    )(plan, *returned)


def shift_by(array, k, places):
    return lax.ppermute(array, "blk", [(i, (i + k) % places) for i in range(places)])


def swap_with(array, q, pieces):
    return lax.ppermute(array, "sub", [(i, i ^ q) for i in range(pieces)])


def after(array, *others):
    return lax.optimization_barrier((array,) + others)[0]


def pattern_path(counts, capacity, pieces, rows, plan, bits, own, slots):
    places = len(counts)
    taken = slots_of(counts, capacity)
    blocks = len(taken)
    per = pieces // 2
    moved = []
    for k, at in taken[capacity:]:
        sent = slots[at - capacity]
        if len(moved) == 2:
            sent = after(sent, moved[0])
        moved.append(shift_by(sent, k, places))
    held = {}
    first = [0] + list(range(capacity, blocks + 1))
    for g, array in enumerate([own] + moved):
        last = g == len(moved)
        across = swap_with(array, 2, pieces)
        beside = swap_with(array, 1, pieces)
        for n, b in enumerate(range(first[g], first[g + 1])):
            held[b, 0], held[b, 1], held[b, 2] = (array, n, rows), (beside, n, rows), (across, n, rows)
        if last:
            runs = range(blocks * per - 1)
            sums, known, lefts = score(pieces, held, range(blocks), runs, [(0, blocks, 0, len(runs))], name="score_most")
            across = after(across, sums)
        corner = swap_with(across, 1, pieces)
        for n, b in enumerate(range(first[g], first[g + 1])):
            held[b, 3] = (corner, n, rows)
    spots = [2 + places * capacity + at for _, at in taken]
    (dense,) = score(pieces, held, range(0), range(blocks * per - 1, blocks * per), [(0, blocks, 0, 1)],
                     (plan, spots, bits, None, [(sums, known)], lefts), name="score_late")
    returned = [dense] + [lax.ppermute(dense, "blk", [(i, i ^ q) for i in range(places)]) for q in range(1, places)]
    return place_rows(taken, capacity, pieces, plan, returned, blocks, rows)


def general_path(capacity, pieces, embeddings, row_count, fetch_list, left, right, pairs):
    places = lax.axis_size("blk")
    me = lax.axis_index("blk")
    sub = lax.axis_index("sub")
    blocks, rows, width = embeddings.shape
    total = places * capacity
    local_ids = jnp.arange(blocks, dtype=jnp.int32)
    slot_ids = jnp.arange(total, dtype=jnp.int32)
    owned = me * blocks + local_ids
    here = fetch_list[:, :, None] == owned[None, None, :]
    scorer = jnp.sum(jnp.where(here, jnp.arange(places, dtype=jnp.int32)[:, None, None], 0), axis=(0, 1))
    same = scorer[:, None] == scorer[None, :]
    rank = jnp.sum(same & (local_ids[None, :] < local_ids[:, None]), axis=1)
    send_slot = scorer * capacity + rank
    placing = send_slot[:, None] == slot_ids[None, :]
    source = jnp.sum(jnp.where(placing, local_ids[:, None], 0), axis=0)
    exchange = lambda x: lax.all_to_all(x, "blk", split_axis=0, concat_axis=0, tiled=True)
    mark = jax.vmap(lambda block, count: block.at[:, :LANES].set(marked(block[:, :LANES], sub, count)))
    incoming = exchange(jnp.take(mark(embeddings, row_count), source, axis=0))
    wanted = lax.dynamic_index_in_dim(fetch_list, me, 0, keepdims=False)
    owner, local = wanted // blocks, wanted % blocks
    together = owner[:, None] == owner[None, :]
    recv_rank = jnp.sum(together & (local[None, :] < local[:, None]), axis=1)
    recv_slot = owner * capacity + recv_rank
    live = jnp.arange(left.shape[1], dtype=jnp.int32) < pairs[0]
    one = jnp.int32(1)
    hot = lambda at: jnp.where(live[:, None], (at[:, None] == jnp.arange(blocks * blocks)).astype(jnp.int32), 0)
    listed = jnp.max(hot(left[0] * blocks + right[0]) | hot(right[0] * blocks + left[0]), axis=0)
    bits = jnp.sum(listed * lax.shift_left(one, jnp.arange(blocks * blocks, dtype=jnp.int32)))
    held = {}
    for b in range(blocks):
        block = lax.dynamic_index_in_dim(incoming, recv_slot[b], 0, keepdims=False)
        for q in range(pieces):
            held[b, q] = (swap_with(block, q, pieces) if q else block), 0, rows
    runs = range(blocks * pieces // 2)
    meta = local_ids, range(blocks), bits[None].astype(jnp.int32), [list(range(blocks))], [], []
    (dense,) = score(pieces, held, range(blocks), runs, [(0, blocks, 0, len(runs))], meta, name="score_all")
    back = (recv_slot[None, :] == slot_ids[:, None]).astype(jnp.float32)
    returned = exchange(jnp.sum(back[:, :, None] * dense[None, :, :], axis=1))
    return jnp.take(returned, send_slot, axis=0)


def body(embeddings, row_count, fetch_list, pair_left, pair_right, pair_count):
    places = lax.axis_size("blk")
    pieces = lax.axis_size("sub")
    blocks = embeddings.shape[0]
    capacity = (blocks + places - 1) // places
    given = (embeddings, row_count, fetch_list, pair_left, pair_right, pair_count)
    general = functools.partial(general_path, capacity, pieces)
    patterns = block_patterns(places, capacity, blocks)
    if not patterns or pieces != 4:
        return general(*given)
    me = lax.axis_index("blk").astype(jnp.int32)[None]
    sub = lax.axis_index("sub").astype(jnp.int32)[None]
    plan, bits, own, slots = make_plan(patterns, places, capacity, me, sub, *given)
    rows = embeddings.shape[1]
    branches = [
        lambda plan, bits, own, slots, given, counts=counts: pattern_path(
            counts, capacity, pieces, rows, plan, bits, own, slots)
        for counts in patterns
    ] + [lambda plan, bits, own, slots, given: general(*given)]
    return lax.switch(plan[0], branches, plan, bits, own, slots, given)


def solution(mesh):
    in_specs = (
        P(("parts", "blk"), "sub", None),
        P(("parts", "blk")),
        P("parts", None),
        P(("parts", "blk"), None),
        P(("parts", "blk"), None),
        P(("parts", "blk")),
    )
    out_specs = P(("parts", "blk"), "sub")
    return jax.shard_map(body, mesh=mesh, in_specs=in_specs, out_specs=out_specs, check_vma=False)
```

```python
import functools
import itertools
import math

import jax
import jax.numpy as jnp
from jax import lax
from jax.experimental import pallas as pl
from jax.experimental.pallas import tpu as pltpu
from jax.sharding import PartitionSpec as P

kernel_scale = 24.0
norm_eps = 1e-06
LANES = 128
FLOPS = 4
UNUSED = 2.0 ** 60
UNUSED_SQUARES = 2.0 ** 100
SCALE_IN_USE = 2.0 ** -30
VMEM_LIMIT = 24 * 1024 * 1024
ANY = pl.BlockSpec(memory_space=pl.ANY)
SMEM = pl.BlockSpec(memory_space=pltpu.SMEM)
VMEM = pl.BlockSpec(memory_space=pltpu.VMEM)


def block_patterns(places, capacity, blocks):
    if capacity < 2 or places > 4:
        return []
    cost = lambda counts: sum(c * min(k, places - k) for k, c in enumerate(counts))
    best = {}
    for counts in itertools.product(range(capacity + 1), repeat=places):
        if sum(counts) != blocks:
            continue
        turns = [counts[t:] + counts[:t] for t in range(places)]
        pick = min(turns, key=lambda c: (-c[0], cost(c), c))
        best[min(turns)] = pick
    return sorted(best.values(), key=cost)


def owner_of(block, blocks, places):
    return sum((block >= i * blocks).astype(jnp.int32) for i in range(1, places))


def slots_of(counts, capacity):
    places = len(counts)
    nearest = sorted((k for k in range(1, places) if counts[k]), key=lambda k: min(k, places - k))
    order = [(0, j) for j in range(counts[0])] + [(k, 0) for k in nearest] + [(k, 1) for k in nearest if counts[k] > 1]
    return [(k, k * capacity + j) for k, j in order]


def unary(counts):
    return sum(((1 << c) - 1) << (2 * r) for r, c in enumerate(counts))


def marked(first_lanes, sub, count):
    rows, lanes = first_lanes.shape
    row = lax.broadcasted_iota(jnp.int32, (rows, lanes), 0) + sub * rows
    lane = lax.broadcasted_iota(jnp.int32, (rows, lanes), 1)
    return jnp.where((row >= count) & (lane == 0), UNUSED, first_lanes.astype(jnp.float32)).astype(first_lanes.dtype)


def plan_kernel(patterns, places, capacity, me_ref, sub_ref, fetch_ref, count_ref, left_ref, right_ref, pairs_ref,
                emb_ref, plan_ref, bits_ref, *rest):
    slots, sems = rest[:-1], rest[-1]
    blocks = count_ref.shape[0]
    rows = emb_ref.shape[1]
    views = [slots[0].at[pl.ds(j * rows, rows)] for j in range(capacity)] + list(slots[1:])
    me = me_ref[0]
    used = jnp.int32(0)
    for s in range(places):
        seen = jnp.int32(0)
        for p in range(blocks):
            owner = owner_of(fetch_ref[s, p], blocks, places)
            turned = owner - s
            bit = lax.shift_left(jnp.int32(1), 2 * jnp.where(turned < 0, turned + places, turned))
            seen = seen | bit | ((seen & bit) << 1)
        used = used | seen
    choice = jnp.int32(len(patterns))
    shift = jnp.int32(0)
    for m in reversed(range(len(patterns))):
        for t in range(places):
            allowed = unary([patterns[m][(t - r) % places] for r in range(places)])
            fits = (used & ~allowed) == 0
            choice = jnp.where(fits, m, choice)
            shift = jnp.where(fits, t, shift)
    plan_ref[0] = choice
    plan_ref[plan_ref.shape[0] - 1] = me
    plan_ref[1] = shift
    mine = lax.rem(me + places - shift, places)
    total = places * capacity
    copies = []
    for k in range(places):
        owner = lax.rem(me + places - k, places)
        target = lax.rem(me + k + places - shift, places)
        place, seen = [jnp.int32(0)] * capacity, jnp.int32(0)
        send, spot, sent = [jnp.int32(0)] * capacity, [jnp.int32(0)] * capacity, jnp.int32(0)
        for p in range(blocks):
            listed = fetch_ref[mine, p]
            hit = owner_of(listed, blocks, places) == owner
            outward = fetch_ref[target, p]
            goes = owner_of(outward, blocks, places) == me
            for j in range(capacity):
                place[j] = jnp.where(hit & (seen == j), p, place[j])
                send[j] = jnp.where(goes & (sent == j), outward - me * blocks, send[j])
                spot[j] = jnp.where(goes & (sent == j), p, spot[j])
            seen = seen + hit.astype(jnp.int32)
            sent = sent + goes.astype(jnp.int32)
        for j in range(capacity):
            at = k * capacity + j
            copy = pltpu.make_async_copy(emb_ref.at[send[j]], views[at], sems.at[at])
            pl.when(sent > j)(copy.start)
            copies.append((sent > j, copy))
            plan_ref[2 + at] = send[j]
            plan_ref[2 + total + at] = place[j]
            plan_ref[2 + 2 * total + at] = spot[j]
    bits = jnp.int32(0)
    for p in range(left_ref.shape[1]):
        a, b = left_ref[0, p], right_ref[0, p]
        both = lax.shift_left(jnp.int32(1), a * blocks + b) | lax.shift_left(jnp.int32(1), b * blocks + a)
        bits = bits | jnp.where(p < pairs_ref[0], both, 0)
    bits_ref[0] = bits
    for at, (filled, copy) in enumerate(copies):
        pl.when(filled)(copy.wait)
        views[at][:, :LANES] = marked(views[at][:, :LANES], sub_ref[0], count_ref[plan_ref[2 + at]])


def make_plan(patterns, places, capacity, me, sub, embeddings, row_count, fetch_list, left, right, pairs):
    blocks, rows, width = embeddings.shape
    total = places * capacity
    slot = jax.ShapeDtypeStruct((rows, width), embeddings.dtype)
    own = jax.ShapeDtypeStruct((capacity * rows, width), embeddings.dtype)
    others = total - capacity
    out = pl.pallas_call(
        functools.partial(plan_kernel, patterns, places, capacity),
        out_shape=[jax.ShapeDtypeStruct((3 + 3 * total,), jnp.int32),
                   jax.ShapeDtypeStruct((1,), jnp.int32), own] + [slot] * others,
        in_specs=[SMEM] * 7 + [ANY],
        out_specs=[SMEM, SMEM] + [VMEM] * (1 + others),
        scratch_shapes=[pltpu.SemaphoreType.DMA((total,))],
        name="plan_and_gather",
    )(me, sub, fetch_list, row_count, left, right, pairs, embeddings)
    return out[0], out[1], out[2], out[3:]


def pairs_of(per, runs, steps):
    return [(a, b) for lo, hi, start, end in steps
            for b in sorted({runs[run] // per for run in range(start, end)}) for a in range(lo, hi)]


def score_kernel(rows, width, pieces, wheres, owned, runs, steps, places, *refs):
    refs = list(refs)
    arrays = [refs.pop(0) for _ in range(1 + max(i for i, _ in wheres))]
    spots_in = [arrays[i].at[pl.ds(n * rows, rows)] for i, n in wheres]
    right_in = spots_in
    finish = passed = None
    if places is not None:
        finish = [refs.pop(0) for _ in range(2 + places[0])]
        if not owned:
            passed = refs.pop(0), refs.pop(0)
    hand_on = places is None
    out_refs = [refs.pop(0) for _ in (places[2] if places and places[2] else range(1 + 2 * hand_on))]
    if hand_on:
        right, gram, right_sems = refs[:3]
        left, left_scale = out_refs[1:]
    elif passed is None:
        left, right, left_scale, gram, right_sems = refs[:5]
    else:
        right, gram, right_sems = refs[:3]
        left, left_scale = passed
    sums = refs[-1] if places else out_refs[0]
    per = pieces // 2
    copies = []
    for i in range(2 * len(runs)):
        copies.append(pltpu.make_async_copy(right_in[i], right.at[pl.ds(i * rows, rows)], right_sems.at[i]))
    for copy in copies:
        copy.start()
    eye = lax.broadcasted_iota(jnp.int32, (rows, rows), 0) == lax.broadcasted_iota(jnp.int32, (rows, rows), 1)

    def squares(block):
        wide = block.astype(jnp.float32)
        return jnp.sum(wide * wide, axis=1, keepdims=True)

    def lanes(col):
        return jnp.sum(jnp.where(eye, col, 0.0), axis=0, keepdims=True)

    @pl.loop(0, len(owned))
    def _(i):
        here = pl.ds(pl.multiple_of(i * rows, rows), rows)
        there = pl.ds(pl.multiple_of(i * pieces * rows, rows), rows)
        pltpu.make_async_copy(right_in[0], right.at[there], right_sems.at[i * pieces]).wait()
        left[here, :] = right[there, :]
        inv = lax.rsqrt(squares(left[here, :]) * (1.0 / width) + norm_eps)
        left_scale[here, :] = jnp.broadcast_to(inv * (kernel_scale / width * math.log2(math.e)), (rows, rows))

    arrived = base = 0
    for lo, hi, start, end in steps:
        fresh = end > arrived
        first_block = runs[start] // per

        @pl.loop(start, end)
        def _(run):
            if fresh:
                for h in range(2):
                    copy = pltpu.make_async_copy(
                        right_in[0], right.at[pl.ds((2 * run + h) * rows, rows)], right_sems.at[2 * run + h])
                    if h == 0 and owned:
                        pl.when(lax.rem(runs[0] + run, per) != 0)(copy.wait)
                    else:
                        copy.wait()
            flat = runs[0] + run
            b = lax.div(flat, per)
            q = 2 * lax.rem(flat, per)
            scale_row, valid = [], []
            for h in range(2):
                here = pl.ds(pl.multiple_of((2 * run + h) * rows, rows), rows)
                total = lanes(squares(right[here, :]))
                scale_row.append(lax.rsqrt(total * (1.0 / width) + norm_eps))
                valid.append((total < UNUSED_SQUARES).astype(jnp.float32))
            both = right[pl.ds(pl.multiple_of(2 * run * rows, rows), 2 * rows), :]
            gram[:(hi - lo) * rows, :] = lax.dot_general(
                left[lo * rows:hi * rows, :], both, (((1,), (1,)), ((), ())), preferred_element_type=jnp.float32)
            for a in range(lo, hi):
                there = slice((a - lo) * rows, (a - lo + 1) * rows)
                scale = left_scale[a * rows:(a + 1) * rows, :]
                same = eye & ((b == a) & (q == 0))
                near = jnp.exp2(gram[there, :rows] * scale * scale_row[0]) * valid[0]
                far = jnp.exp2(gram[there, rows:] * scale * scale_row[1]) * valid[1]
                tile = jnp.where(same, 0.0, near) + far
                pair = base + (b - first_block) * (hi - lo) + a - lo
                if end - start > 1:
                    tile = tile + jnp.where(q == 0, 0.0, sums[pair])
                sums[pair] = tile

        arrived = max(arrived, end)
        base += (runs[end - 1] // per + 1 - first_block) * (hi - lo)
    if places is None:
        return
    count, spots, groups, listed = places
    plan_ref, bits_ref = finish[:2]
    bits = bits_ref[0]
    spot = [plan_ref[at] for at in spots]
    blocks = len(spots)
    if groups is None:
        for a in range(blocks):
            in_use = left_scale[a * rows:(a + 1) * rows, :] > SCALE_IN_USE
            by_block = {}
            for source, at, b in listed[a]:
                part = (sums if source < 0 else finish[2 + source])[at]
                by_block[b] = by_block[b] + part if b in by_block else part
            for b, part in by_block.items():
                total = jnp.sum(jnp.transpose(jnp.where(in_use, part, 0.0)), axis=0, keepdims=True)
                out_refs[0][pl.ds(a * blocks + spot[b], 1), :] = total
        lane = lax.broadcasted_iota(jnp.int32, (1, rows), 1)
        flags = sum(jnp.where(lane == i, (bits >> i) & 1, 0) for i in range(blocks * blocks))
        out_refs[0][blocks * blocks:blocks * blocks + 1, :] = flags.astype(jnp.float32)
        return
    for ref, group in zip(out_refs, groups):
        for n, a in enumerate(group):
            total = jnp.zeros((rows, rows), jnp.float32)
            for source, at, right_block in listed[a]:
                paired = (bits >> (spot[a] * blocks + spot[right_block])) & 1
                total = total + (sums if source < 0 else finish[2 + source])[at] * paired.astype(jnp.float32)
            total = jnp.sum(total, axis=1, keepdims=True)
            total = jnp.where(left_scale[a * rows:(a + 1) * rows, :1] > SCALE_IN_USE, total, 0.0)
            ref[n:n + 1, :] = jnp.log1p(lanes(total) / (pieces * rows))


def score(pieces, held, owned, runs, steps, meta=None, name="score"):
    array, _, rows = next(iter(held.values()))
    width = array.shape[1]
    per = pieces // 2
    rights = [held[run // per, 2 * (run % per) + h] for run in runs for h in range(2)]
    arrays, wheres = [], []
    for array, n, _ in rights:
        known = [i for i, other in enumerate(arrays) if other is array]
        if not known:
            arrays.append(array)
        wheres.append((known[0] if known else len(arrays) - 1, n))
    tall = max(hi - lo for lo, hi, _, _ in steps) * rows
    pairs = pairs_of(per, runs, steps)
    sums = jax.ShapeDtypeStruct((len(pairs), rows, rows), jnp.float32)
    tall_left = len(owned) * rows
    lefts = [(tall_left, width), jnp.bfloat16], [(tall_left, rows), jnp.float32]
    places, extra, extra_specs, out_shape, scratch = None, [], [], [sums] + [jax.ShapeDtypeStruct(*x) for x in lefts], []
    if meta is not None:
        plan, spots, bits, groups, earlier, passed = meta
        listed = [[] for _ in spots]
        for source, (_, known) in enumerate(earlier + [(None, pairs)]):
            for at, (a, b) in enumerate(known):
                listed[a].append((source if source < len(earlier) else -1, at, b))
        places = len(earlier), spots, groups, listed
        extra = [plan, bits] + [array for array, _ in earlier] + list(passed)
        extra_specs = [SMEM, SMEM] + [VMEM] * (len(earlier) + len(passed))
        count = -(-(len(spots) ** 2 + 1) // 8) * 8
        out_shape = [jax.ShapeDtypeStruct((len(g), rows), jnp.float32) for g in groups or [range(count)]]
        scratch = [pltpu.VMEM(sums.shape, jnp.float32)]
    keeps = meta is not None and owned
    flops = sum(4 * (hi - lo) * (end - start) * rows * rows * width for lo, hi, start, end in steps)
    moved = (len(owned) + len(rights)) * rows * width * 2
    result = pl.pallas_call(
        functools.partial(score_kernel, rows, width, pieces, wheres, owned, runs, steps, places),
        out_shape=out_shape,
        in_specs=[ANY] * len(arrays) + extra_specs,
        out_specs=[VMEM] * len(out_shape),
        scratch_shapes=([pltpu.VMEM(*lefts[0])] if keeps else []) + [
            pltpu.VMEM((len(rights) * rows, width), jnp.bfloat16)] + ([pltpu.VMEM(*lefts[1])] if keeps else []) + [
            pltpu.VMEM((tall, 2 * rows), jnp.float32),
            pltpu.SemaphoreType.DMA((len(rights),)),
        ] + scratch,
        compiler_params=pltpu.CompilerParams(vmem_limit_bytes=VMEM_LIMIT),
        cost_estimate=pl.CostEstimate(flops=0, bytes_accessed=0, transcendentals=0),
        name=name,
    )(*arrays, *extra)
    return (result[0], pairs, result[1:]) if meta is None else result


def place_kernel(taken, capacity, pieces, plan_ref, *refs):
    refs, out_ref, held = refs[:-2], refs[-2], refs[-1]
    places = len(refs)
    blocks, rows = out_ref.shape
    total = places * capacity
    me = plan_ref[plan_ref.shape[0] - 1]
    for q, ref in enumerate(refs):
        held[places - 1 - q] = ref[...]
    lane = lax.broadcasted_iota(jnp.int32, (blocks, rows), 1)
    spot = lax.broadcasted_iota(jnp.int32, (blocks, rows), 0)
    for n, (k, at) in enumerate(taken):
        scorer = lax.rem(me + k, places)
        group = lax.rem(scorer + places - plan_ref[1], places)
        flags = held[me ^ group, blocks * blocks:blocks * blocks + 1, :]
        first = plan_ref[2 + 2 * total + at] * blocks
        paired = jnp.sum(jnp.where(lane == spot + first, flags, 0.0), axis=1, keepdims=True)
        sums = held[me ^ scorer, n * blocks:(n + 1) * blocks, :]
        sums = jnp.sum(jnp.where(paired > 0.0, sums, 0.0), axis=0, keepdims=True)
        out_ref[pl.ds(plan_ref[2 + at], 1), :] = jnp.log1p(sums / (pieces * rows))


def place_rows(taken, capacity, pieces, plan, returned, blocks, rows):
    return pl.pallas_call(
        functools.partial(place_kernel, taken, capacity, pieces),
        out_shape=jax.ShapeDtypeStruct((blocks, rows), jnp.float32),
        in_specs=[SMEM] + [VMEM] * len(returned),
        out_specs=VMEM,
        scratch_shapes=[pltpu.VMEM((len(returned),) + returned[0].shape, jnp.float32)],
        name="place_rows",
    )(plan, *returned)


def shift_by(array, k, places):
    return lax.ppermute(array, "blk", [(i, (i + k) % places) for i in range(places)])


def swap_with(array, q, pieces):
    return lax.ppermute(array, "sub", [(i, i ^ q) for i in range(pieces)])


def after(array, *others):
    return lax.optimization_barrier((array,) + others)[0]


def pattern_path(counts, capacity, pieces, rows, plan, bits, own, slots):
    places = len(counts)
    taken = slots_of(counts, capacity)
    blocks = len(taken)
    per = pieces // 2
    moved = []
    for k, at in taken[capacity:]:
        sent = slots[at - capacity]
        if len(moved) == 2:
            sent = after(sent, *(moved if counts[places // 2] > 1 else moved[1:]))
        moved.append(shift_by(sent, k, places))
    held = {}
    first = [0] + list(range(capacity, blocks + 1))
    for g, array in enumerate([own] + moved):
        last = g == len(moved)
        across = swap_with(array, 2, pieces)
        beside = swap_with(array, 1, pieces)
        for n, b in enumerate(range(first[g], first[g + 1])):
            held[b, 0], held[b, 1], held[b, 2] = (array, n, rows), (beside, n, rows), (across, n, rows)
        if last:
            runs = range(blocks * per - 1)
            sums, known, lefts = score(pieces, held, range(blocks), runs, [(0, blocks, 0, len(runs))], name="score_most")
            across = after(across, sums)
        corner = swap_with(across, 1, pieces)
        for n, b in enumerate(range(first[g], first[g + 1])):
            held[b, 3] = (corner, n, rows)
    spots = [2 + places * capacity + at for _, at in taken]
    (dense,) = score(pieces, held, range(0), range(blocks * per - 1, blocks * per), [(0, blocks, 0, 1)],
                     (plan, spots, bits, None, [(sums, known)], lefts), name="score_late")
    returned = {0: dense}
    for q in reversed(range(1, places)):
        returned[q] = lax.ppermute(dense, "blk", [(i, i ^ q) for i in range(places)])
    returned = [returned[q] for q in reversed(range(places))]
    return place_rows(taken, capacity, pieces, plan, returned, blocks, rows)


def general_path(capacity, pieces, embeddings, row_count, fetch_list, left, right, pairs):
    places = lax.axis_size("blk")
    me = lax.axis_index("blk")
    sub = lax.axis_index("sub")
    blocks, rows, width = embeddings.shape
    total = places * capacity
    local_ids = jnp.arange(blocks, dtype=jnp.int32)
    slot_ids = jnp.arange(total, dtype=jnp.int32)
    owned = me * blocks + local_ids
    here = fetch_list[:, :, None] == owned[None, None, :]
    scorer = jnp.sum(jnp.where(here, jnp.arange(places, dtype=jnp.int32)[:, None, None], 0), axis=(0, 1))
    same = scorer[:, None] == scorer[None, :]
    rank = jnp.sum(same & (local_ids[None, :] < local_ids[:, None]), axis=1)
    send_slot = scorer * capacity + rank
    placing = send_slot[:, None] == slot_ids[None, :]
    source = jnp.sum(jnp.where(placing, local_ids[:, None], 0), axis=0)
    exchange = lambda x: lax.all_to_all(x, "blk", split_axis=0, concat_axis=0, tiled=True)
    mark = jax.vmap(lambda block, count: block.at[:, :LANES].set(marked(block[:, :LANES], sub, count)))
    incoming = exchange(jnp.take(mark(embeddings, row_count), source, axis=0))
    wanted = lax.dynamic_index_in_dim(fetch_list, me, 0, keepdims=False)
    owner, local = wanted // blocks, wanted % blocks
    together = owner[:, None] == owner[None, :]
    recv_rank = jnp.sum(together & (local[None, :] < local[:, None]), axis=1)
    recv_slot = owner * capacity + recv_rank
    live = jnp.arange(left.shape[1], dtype=jnp.int32) < pairs[0]
    one = jnp.int32(1)
    hot = lambda at: jnp.where(live[:, None], (at[:, None] == jnp.arange(blocks * blocks)).astype(jnp.int32), 0)
    listed = jnp.max(hot(left[0] * blocks + right[0]) | hot(right[0] * blocks + left[0]), axis=0)
    bits = jnp.sum(listed * lax.shift_left(one, jnp.arange(blocks * blocks, dtype=jnp.int32)))
    held = {}
    for b in range(blocks):
        block = lax.dynamic_index_in_dim(incoming, recv_slot[b], 0, keepdims=False)
        for q in range(pieces):
            held[b, q] = (swap_with(block, q, pieces) if q else block), 0, rows
    runs = range(blocks * pieces // 2)
    meta = local_ids, range(blocks), bits[None].astype(jnp.int32), [list(range(blocks))], [], []
    (dense,) = score(pieces, held, range(blocks), runs, [(0, blocks, 0, len(runs))], meta, name="score_all")
    back = (recv_slot[None, :] == slot_ids[:, None]).astype(jnp.float32)
    returned = exchange(jnp.sum(back[:, :, None] * dense[None, :, :], axis=1))
    return jnp.take(returned, send_slot, axis=0)


def body(embeddings, row_count, fetch_list, pair_left, pair_right, pair_count):
    places = lax.axis_size("blk")
    pieces = lax.axis_size("sub")
    blocks = embeddings.shape[0]
    capacity = (blocks + places - 1) // places
    given = (embeddings, row_count, fetch_list, pair_left, pair_right, pair_count)
    general = functools.partial(general_path, capacity, pieces)
    patterns = block_patterns(places, capacity, blocks)
    if not patterns or pieces != 4:
        return general(*given)
    me = lax.axis_index("blk").astype(jnp.int32)[None]
    sub = lax.axis_index("sub").astype(jnp.int32)[None]
    plan, bits, own, slots = make_plan(patterns, places, capacity, me, sub, *given)
    rows = embeddings.shape[1]
    branches = [
        lambda plan, bits, own, slots, given, counts=counts: pattern_path(
            counts, capacity, pieces, rows, plan, bits, own, slots)
        for counts in patterns
    ] + [lambda plan, bits, own, slots, given: general(*given)]
    return lax.switch(plan[0], branches, plan, bits, own, slots, given)


def solution(mesh):
    in_specs = (
        P(("parts", "blk"), "sub", None),
        P(("parts", "blk")),
        P("parts", None),
        P(("parts", "blk"), None),
        P(("parts", "blk"), None),
        P(("parts", "blk")),
    )
    out_specs = P(("parts", "blk"), "sub")
    return jax.shard_map(body, mesh=mesh, in_specs=in_specs, out_specs=out_specs, check_vma=False)
```

```python
import functools
import itertools
import math

import jax
import jax.numpy as jnp
from jax import lax
from jax.experimental import pallas as pl
from jax.experimental.pallas import tpu as pltpu
from jax.sharding import PartitionSpec as P

kernel_scale = 24.0
norm_eps = 1e-06
LANES = 128
FLOPS = 4
UNUSED = 2.0 ** 60
UNUSED_SQUARES = 2.0 ** 100
SCALE_IN_USE = 2.0 ** -30
VMEM_LIMIT = 24 * 1024 * 1024
ANY = pl.BlockSpec(memory_space=pl.ANY)
SMEM = pl.BlockSpec(memory_space=pltpu.SMEM)
VMEM = pl.BlockSpec(memory_space=pltpu.VMEM)


def block_patterns(places, capacity, blocks):
    if capacity < 2 or places > 4:
        return []
    cost = lambda counts: sum(c * min(k, places - k) for k, c in enumerate(counts))
    best = {}
    for counts in itertools.product(range(capacity + 1), repeat=places):
        if sum(counts) != blocks:
            continue
        turns = [counts[t:] + counts[:t] for t in range(places)]
        pick = min(turns, key=lambda c: (-c[0], cost(c), c))
        best[min(turns)] = pick
    return sorted(best.values(), key=cost)


def owner_of(block, blocks, places):
    return sum((block >= i * blocks).astype(jnp.int32) for i in range(1, places))


def slots_of(counts, capacity):
    places = len(counts)
    nearest = sorted((k for k in range(1, places) if counts[k]), key=lambda k: min(k, places - k))
    order = [(0, j) for j in range(counts[0])] + [(k, 0) for k in nearest] + [(k, 1) for k in nearest if counts[k] > 1]
    return [(k, k * capacity + j) for k, j in order]


def unary(counts):
    return sum(((1 << c) - 1) << (2 * r) for r, c in enumerate(counts))


def marked(first_lanes, sub, count):
    rows, lanes = first_lanes.shape
    row = lax.broadcasted_iota(jnp.int32, (rows, lanes), 0) + sub * rows
    lane = lax.broadcasted_iota(jnp.int32, (rows, lanes), 1)
    return jnp.where((row >= count) & (lane == 0), UNUSED, first_lanes.astype(jnp.float32)).astype(first_lanes.dtype)


def plan_kernel(patterns, places, capacity, me_ref, sub_ref, fetch_ref, count_ref, left_ref, right_ref, pairs_ref,
                emb_ref, plan_ref, bits_ref, *rest):
    slots, sems = rest[:-1], rest[-1]
    blocks = count_ref.shape[0]
    rows = emb_ref.shape[1]
    views = [slots[0].at[pl.ds(j * rows, rows)] for j in range(capacity)] + list(slots[1:])
    me = me_ref[0]
    used = jnp.int32(0)
    for s in range(places):
        seen = jnp.int32(0)
        for p in range(blocks):
            owner = owner_of(fetch_ref[s, p], blocks, places)
            turned = owner - s
            bit = lax.shift_left(jnp.int32(1), 2 * jnp.where(turned < 0, turned + places, turned))
            seen = seen | bit | ((seen & bit) << 1)
        used = used | seen
    choice = jnp.int32(len(patterns))
    shift = jnp.int32(0)
    for m in reversed(range(len(patterns))):
        for t in range(places):
            allowed = unary([patterns[m][(t - r) % places] for r in range(places)])
            fits = (used & ~allowed) == 0
            choice = jnp.where(fits, m, choice)
            shift = jnp.where(fits, t, shift)
    plan_ref[0] = choice
    plan_ref[plan_ref.shape[0] - 1] = me
    plan_ref[1] = shift
    mine = lax.rem(me + places - shift, places)
    total = places * capacity
    copies = []
    for k in range(places):
        owner = lax.rem(me + places - k, places)
        target = lax.rem(me + k + places - shift, places)
        place, seen = [jnp.int32(0)] * capacity, jnp.int32(0)
        send, spot, sent = [jnp.int32(0)] * capacity, [jnp.int32(0)] * capacity, jnp.int32(0)
        for p in range(blocks):
            listed = fetch_ref[mine, p]
            hit = owner_of(listed, blocks, places) == owner
            outward = fetch_ref[target, p]
            goes = owner_of(outward, blocks, places) == me
            for j in range(capacity):
                place[j] = jnp.where(hit & (seen == j), p, place[j])
                send[j] = jnp.where(goes & (sent == j), outward - me * blocks, send[j])
                spot[j] = jnp.where(goes & (sent == j), p, spot[j])
            seen = seen + hit.astype(jnp.int32)
            sent = sent + goes.astype(jnp.int32)
        for j in range(capacity):
            at = k * capacity + j
            copy = pltpu.make_async_copy(emb_ref.at[send[j]], views[at], sems.at[at])
            pl.when(sent > j)(copy.start)
            copies.append((sent > j, copy))
            plan_ref[2 + at] = send[j]
            plan_ref[2 + total + at] = place[j]
            plan_ref[2 + 2 * total + at] = spot[j]
    bits = jnp.int32(0)
    for p in range(left_ref.shape[1]):
        a, b = left_ref[0, p], right_ref[0, p]
        both = lax.shift_left(jnp.int32(1), a * blocks + b) | lax.shift_left(jnp.int32(1), b * blocks + a)
        bits = bits | jnp.where(p < pairs_ref[0], both, 0)
    bits_ref[0] = bits
    for at, (filled, copy) in enumerate(copies):
        pl.when(filled)(copy.wait)
        views[at][:, :LANES] = marked(views[at][:, :LANES], sub_ref[0], count_ref[plan_ref[2 + at]])


def make_plan(patterns, places, capacity, me, sub, embeddings, row_count, fetch_list, left, right, pairs):
    blocks, rows, width = embeddings.shape
    total = places * capacity
    slot = jax.ShapeDtypeStruct((rows, width), embeddings.dtype)
    own = jax.ShapeDtypeStruct((capacity * rows, width), embeddings.dtype)
    others = total - capacity
    out = pl.pallas_call(
        functools.partial(plan_kernel, patterns, places, capacity),
        out_shape=[jax.ShapeDtypeStruct((3 + 3 * total,), jnp.int32),
                   jax.ShapeDtypeStruct((1,), jnp.int32), own] + [slot] * others,
        in_specs=[SMEM] * 7 + [ANY],
        out_specs=[SMEM, SMEM] + [VMEM] * (1 + others),
        scratch_shapes=[pltpu.SemaphoreType.DMA((total,))],
        name="plan_and_gather",
    )(me, sub, fetch_list, row_count, left, right, pairs, embeddings)
    return out[0], out[1], out[2], out[3:]


def pairs_of(per, runs, steps):
    return [(a, b) for lo, hi, start, end in steps
            for b in sorted({runs[run] // per for run in range(start, end)}) for a in range(lo, hi)]


def score_kernel(rows, width, pieces, wheres, owned, runs, steps, places, *refs):
    refs = list(refs)
    arrays = [refs.pop(0) for _ in range(1 + max(i for i, _ in wheres))]
    spots_in = [arrays[i].at[pl.ds(n * rows, rows)] for i, n in wheres]
    right_in = spots_in
    finish = passed = None
    if places is not None:
        finish = [refs.pop(0) for _ in range(2 + places[0])]
        if not owned:
            passed = refs.pop(0), refs.pop(0)
    hand_on = places is None
    out_refs = [refs.pop(0) for _ in (places[2] if places and places[2] else range(1 + 2 * hand_on))]
    if hand_on:
        right, gram, right_sems = refs[:3]
        left, left_scale = out_refs[1:]
    elif passed is None:
        left, right, left_scale, gram, right_sems = refs[:5]
    else:
        right, gram, right_sems = refs[:3]
        left, left_scale = passed
    sums = refs[-1] if places else out_refs[0]
    per = pieces // 2
    copies = []
    for i in range(2 * len(runs)):
        copies.append(pltpu.make_async_copy(right_in[i], right.at[pl.ds(i * rows, rows)], right_sems.at[i]))
    for copy in copies:
        copy.start()
    eye = lax.broadcasted_iota(jnp.int32, (rows, rows), 0) == lax.broadcasted_iota(jnp.int32, (rows, rows), 1)

    def squares(block):
        wide = block.astype(jnp.float32)
        return jnp.sum(wide * wide, axis=1, keepdims=True)

    def lanes(col):
        return jnp.sum(jnp.where(eye, col, 0.0), axis=0, keepdims=True)

    @pl.loop(0, len(owned))
    def _(i):
        here = pl.ds(pl.multiple_of(i * rows, rows), rows)
        there = pl.ds(pl.multiple_of(i * pieces * rows, rows), rows)
        pltpu.make_async_copy(right_in[0], right.at[there], right_sems.at[i * pieces]).wait()
        left[here, :] = right[there, :]
        inv = lax.rsqrt(squares(left[here, :]) * (1.0 / width) + norm_eps)
        left_scale[here, :] = jnp.broadcast_to(inv * (kernel_scale / width * math.log2(math.e)), (rows, rows))

    arrived = base = 0
    for lo, hi, start, end in steps:
        fresh = end > arrived
        first_block = runs[start] // per

        @pl.loop(start, end)
        def _(run):
            if fresh:
                for h in range(2):
                    copy = pltpu.make_async_copy(
                        right_in[0], right.at[pl.ds((2 * run + h) * rows, rows)], right_sems.at[2 * run + h])
                    if h == 0 and owned:
                        pl.when(lax.rem(runs[0] + run, per) != 0)(copy.wait)
                    else:
                        copy.wait()
            flat = runs[0] + run
            b = lax.div(flat, per)
            q = 2 * lax.rem(flat, per)
            scale_row, valid = [], []
            for h in range(2):
                here = pl.ds(pl.multiple_of((2 * run + h) * rows, rows), rows)
                total = lanes(squares(right[here, :]))
                scale_row.append(lax.rsqrt(total * (1.0 / width) + norm_eps))
                valid.append((total < UNUSED_SQUARES).astype(jnp.float32))
            both = right[pl.ds(pl.multiple_of(2 * run * rows, rows), 2 * rows), :]
            gram[:(hi - lo) * rows, :] = lax.dot_general(
                left[lo * rows:hi * rows, :], both, (((1,), (1,)), ((), ())), preferred_element_type=jnp.float32)
            for a in range(lo, hi):
                there = slice((a - lo) * rows, (a - lo + 1) * rows)
                scale = left_scale[a * rows:(a + 1) * rows, :]
                same = eye & ((b == a) & (q == 0))
                near = jnp.exp2(gram[there, :rows] * scale * scale_row[0]) * valid[0]
                far = jnp.exp2(gram[there, rows:] * scale * scale_row[1]) * valid[1]
                tile = jnp.where(same, 0.0, near) + far
                pair = base + (b - first_block) * (hi - lo) + a - lo
                if end - start > 1:
                    tile = tile + jnp.where(q == 0, 0.0, sums[pair])
                sums[pair] = tile

        arrived = max(arrived, end)
        base += (runs[end - 1] // per + 1 - first_block) * (hi - lo)
    if places is None:
        return
    count, spots, groups, listed = places
    plan_ref, bits_ref = finish[:2]
    bits = bits_ref[0]
    spot = [plan_ref[at] for at in spots]
    blocks = len(spots)
    if groups is None:
        for a in range(blocks):
            in_use = left_scale[a * rows:(a + 1) * rows, :] > SCALE_IN_USE
            by_block = {}
            for source, at, b in listed[a]:
                part = (sums if source < 0 else finish[2 + source])[at]
                by_block[b] = by_block[b] + part if b in by_block else part
            for b, part in by_block.items():
                total = jnp.sum(jnp.transpose(jnp.where(in_use, part, 0.0)), axis=0, keepdims=True)
                out_refs[0][pl.ds(a * blocks + spot[b], 1), :] = total
        lane = lax.broadcasted_iota(jnp.int32, (1, rows), 1)
        flags = sum(jnp.where(lane == i, (bits >> i) & 1, 0) for i in range(blocks * blocks))
        out_refs[0][blocks * blocks:blocks * blocks + 1, :] = flags.astype(jnp.float32)
        return
    for ref, group in zip(out_refs, groups):
        for n, a in enumerate(group):
            total = jnp.zeros((rows, rows), jnp.float32)
            for source, at, right_block in listed[a]:
                paired = (bits >> (spot[a] * blocks + spot[right_block])) & 1
                total = total + (sums if source < 0 else finish[2 + source])[at] * paired.astype(jnp.float32)
            total = jnp.sum(total, axis=1, keepdims=True)
            total = jnp.where(left_scale[a * rows:(a + 1) * rows, :1] > SCALE_IN_USE, total, 0.0)
            ref[n:n + 1, :] = jnp.log1p(lanes(total) / (pieces * rows))


def score(pieces, held, owned, runs, steps, meta=None, name="score"):
    array, _, rows = next(iter(held.values()))
    width = array.shape[1]
    per = pieces // 2
    rights = [held[run // per, 2 * (run % per) + h] for run in runs for h in range(2)]
    arrays, wheres = [], []
    for array, n, _ in rights:
        known = [i for i, other in enumerate(arrays) if other is array]
        if not known:
            arrays.append(array)
        wheres.append((known[0] if known else len(arrays) - 1, n))
    tall = max(hi - lo for lo, hi, _, _ in steps) * rows
    pairs = pairs_of(per, runs, steps)
    sums = jax.ShapeDtypeStruct((len(pairs), rows, rows), jnp.float32)
    tall_left = len(owned) * rows
    lefts = [(tall_left, width), jnp.bfloat16], [(tall_left, rows), jnp.float32]
    places, extra, extra_specs, out_shape, scratch = None, [], [], [sums] + [jax.ShapeDtypeStruct(*x) for x in lefts], []
    if meta is not None:
        plan, spots, bits, groups, earlier, passed = meta
        listed = [[] for _ in spots]
        for source, (_, known) in enumerate(earlier + [(None, pairs)]):
            for at, (a, b) in enumerate(known):
                listed[a].append((source if source < len(earlier) else -1, at, b))
        places = len(earlier), spots, groups, listed
        extra = [plan, bits] + [array for array, _ in earlier] + list(passed)
        extra_specs = [SMEM, SMEM] + [VMEM] * (len(earlier) + len(passed))
        count = -(-(len(spots) ** 2 + 1) // 8) * 8
        out_shape = [jax.ShapeDtypeStruct((len(g), rows), jnp.float32) for g in groups or [range(count)]]
        scratch = [pltpu.VMEM(sums.shape, jnp.float32)]
    keeps = meta is not None and owned
    flops = sum(4 * (hi - lo) * (end - start) * rows * rows * width for lo, hi, start, end in steps)
    moved = (len(owned) + len(rights)) * rows * width * 2
    result = pl.pallas_call(
        functools.partial(score_kernel, rows, width, pieces, wheres, owned, runs, steps, places),
        out_shape=out_shape,
        in_specs=[ANY] * len(arrays) + extra_specs,
        out_specs=[VMEM] * len(out_shape),
        scratch_shapes=([pltpu.VMEM(*lefts[0])] if keeps else []) + [
            pltpu.VMEM((len(rights) * rows, width), jnp.bfloat16)] + ([pltpu.VMEM(*lefts[1])] if keeps else []) + [
            pltpu.VMEM((tall, 2 * rows), jnp.float32),
            pltpu.SemaphoreType.DMA((len(rights),)),
        ] + scratch,
        compiler_params=pltpu.CompilerParams(vmem_limit_bytes=VMEM_LIMIT),
        cost_estimate=pl.CostEstimate(flops=0, bytes_accessed=0, transcendentals=0),
        name=name,
    )(*arrays, *extra)
    return (result[0], pairs, result[1:]) if meta is None else result


def place_kernel(taken, capacity, pieces, plan_ref, *refs):
    refs, out_ref, held = refs[:-2], refs[-2], refs[-1]
    places = len(refs)
    blocks, rows = out_ref.shape
    total = places * capacity
    me = plan_ref[plan_ref.shape[0] - 1]
    for q, ref in enumerate(refs):
        held[places - 1 - q] = ref[...]
    lane = lax.broadcasted_iota(jnp.int32, (blocks, rows), 1)
    spot = lax.broadcasted_iota(jnp.int32, (blocks, rows), 0)
    for n, (k, at) in enumerate(taken):
        scorer = lax.rem(me + k, places)
        group = lax.rem(scorer + places - plan_ref[1], places)
        flags = held[me ^ group, blocks * blocks:blocks * blocks + 1, :]
        first = plan_ref[2 + 2 * total + at] * blocks
        paired = jnp.sum(jnp.where(lane == spot + first, flags, 0.0), axis=1, keepdims=True)
        sums = held[me ^ scorer, n * blocks:(n + 1) * blocks, :]
        sums = jnp.sum(jnp.where(paired > 0.0, sums, 0.0), axis=0, keepdims=True)
        out_ref[pl.ds(plan_ref[2 + at], 1), :] = jnp.log1p(sums / (pieces * rows))


def place_rows(taken, capacity, pieces, plan, returned, blocks, rows):
    return pl.pallas_call(
        functools.partial(place_kernel, taken, capacity, pieces),
        out_shape=jax.ShapeDtypeStruct((blocks, rows), jnp.float32),
        in_specs=[SMEM] + [VMEM] * len(returned),
        out_specs=VMEM,
        scratch_shapes=[pltpu.VMEM((len(returned),) + returned[0].shape, jnp.float32)],
        name="place_rows",
    )(plan, *returned)


def shift_by(array, k, places):
    return lax.ppermute(array, "blk", [(i, (i + k) % places) for i in range(places)])


def swap_with(array, q, pieces):
    return lax.ppermute(array, "sub", [(i, i ^ q) for i in range(pieces)])


def after(array, *others):
    return lax.optimization_barrier((array,) + others)[0]


def pattern_path(counts, capacity, pieces, rows, plan, bits, own, slots):
    places = len(counts)
    taken = slots_of(counts, capacity)
    blocks = len(taken)
    per = pieces // 2
    moved = []
    for k, at in taken[capacity:]:
        sent = slots[at - capacity]
        if len(moved) == 2:
            sent = after(sent, *(moved if counts[places // 2] > 1 else moved[1:]))
        moved.append(shift_by(sent, k, places))
    held = {}
    first = [0] + list(range(capacity, blocks + 1))
    for g, array in enumerate([own] + moved):
        last = g == len(moved)
        before, across = across if g else None, swap_with(array, 2, pieces)
        beside = swap_with(after(array, before) if last else array, 1, pieces)
        for n, b in enumerate(range(first[g], first[g + 1])):
            held[b, 0], held[b, 1], held[b, 2] = (array, n, rows), (beside, n, rows), (across, n, rows)
        if last:
            runs = range(blocks * per - 1)
            sums, known, lefts = score(pieces, held, range(blocks), runs, [(0, blocks, 0, len(runs))], name="score_most")
            across = after(across, sums)
        corner = swap_with(across, 1, pieces)
        for n, b in enumerate(range(first[g], first[g + 1])):
            held[b, 3] = (corner, n, rows)
    spots = [2 + places * capacity + at for _, at in taken]
    (dense,) = score(pieces, held, range(0), range(blocks * per - 1, blocks * per), [(0, blocks, 0, 1)],
                     (plan, spots, bits, None, [(sums, known)], lefts), name="score_late")
    returned = {0: dense}
    for q in reversed(range(1, places)):
        returned[q] = lax.ppermute(dense, "blk", [(i, i ^ q) for i in range(places)])
    returned = [returned[q] for q in reversed(range(places))]
    return place_rows(taken, capacity, pieces, plan, returned, blocks, rows)


def general_path(capacity, pieces, embeddings, row_count, fetch_list, left, right, pairs):
    places = lax.axis_size("blk")
    me = lax.axis_index("blk")
    sub = lax.axis_index("sub")
    blocks, rows, width = embeddings.shape
    total = places * capacity
    local_ids = jnp.arange(blocks, dtype=jnp.int32)
    slot_ids = jnp.arange(total, dtype=jnp.int32)
    owned = me * blocks + local_ids
    here = fetch_list[:, :, None] == owned[None, None, :]
    scorer = jnp.sum(jnp.where(here, jnp.arange(places, dtype=jnp.int32)[:, None, None], 0), axis=(0, 1))
    same = scorer[:, None] == scorer[None, :]
    rank = jnp.sum(same & (local_ids[None, :] < local_ids[:, None]), axis=1)
    send_slot = scorer * capacity + rank
    placing = send_slot[:, None] == slot_ids[None, :]
    source = jnp.sum(jnp.where(placing, local_ids[:, None], 0), axis=0)
    exchange = lambda x: lax.all_to_all(x, "blk", split_axis=0, concat_axis=0, tiled=True)
    mark = jax.vmap(lambda block, count: block.at[:, :LANES].set(marked(block[:, :LANES], sub, count)))
    incoming = exchange(jnp.take(mark(embeddings, row_count), source, axis=0))
    wanted = lax.dynamic_index_in_dim(fetch_list, me, 0, keepdims=False)
    owner, local = wanted // blocks, wanted % blocks
    together = owner[:, None] == owner[None, :]
    recv_rank = jnp.sum(together & (local[None, :] < local[:, None]), axis=1)
    recv_slot = owner * capacity + recv_rank
    live = jnp.arange(left.shape[1], dtype=jnp.int32) < pairs[0]
    one = jnp.int32(1)
    hot = lambda at: jnp.where(live[:, None], (at[:, None] == jnp.arange(blocks * blocks)).astype(jnp.int32), 0)
    listed = jnp.max(hot(left[0] * blocks + right[0]) | hot(right[0] * blocks + left[0]), axis=0)
    bits = jnp.sum(listed * lax.shift_left(one, jnp.arange(blocks * blocks, dtype=jnp.int32)))
    held = {}
    for b in range(blocks):
        block = lax.dynamic_index_in_dim(incoming, recv_slot[b], 0, keepdims=False)
        for q in range(pieces):
            held[b, q] = (swap_with(block, q, pieces) if q else block), 0, rows
    runs = range(blocks * pieces // 2)
    meta = local_ids, range(blocks), bits[None].astype(jnp.int32), [list(range(blocks))], [], []
    (dense,) = score(pieces, held, range(blocks), runs, [(0, blocks, 0, len(runs))], meta, name="score_all")
    back = (recv_slot[None, :] == slot_ids[:, None]).astype(jnp.float32)
    returned = exchange(jnp.sum(back[:, :, None] * dense[None, :, :], axis=1))
    return jnp.take(returned, send_slot, axis=0)


def body(embeddings, row_count, fetch_list, pair_left, pair_right, pair_count):
    places = lax.axis_size("blk")
    pieces = lax.axis_size("sub")
    blocks = embeddings.shape[0]
    capacity = (blocks + places - 1) // places
    given = (embeddings, row_count, fetch_list, pair_left, pair_right, pair_count)
    general = functools.partial(general_path, capacity, pieces)
    patterns = block_patterns(places, capacity, blocks)
    if not patterns or pieces != 4:
        return general(*given)
    me = lax.axis_index("blk").astype(jnp.int32)[None]
    sub = lax.axis_index("sub").astype(jnp.int32)[None]
    plan, bits, own, slots = make_plan(patterns, places, capacity, me, sub, *given)
    rows = embeddings.shape[1]
    branches = [
        lambda plan, bits, own, slots, given, counts=counts: pattern_path(
            counts, capacity, pieces, rows, plan, bits, own, slots)
        for counts in patterns
    ] + [lambda plan, bits, own, slots, given: general(*given)]
    return lax.switch(plan[0], branches, plan, bits, own, slots, given)


def solution(mesh):
    in_specs = (
        P(("parts", "blk"), "sub", None),
        P(("parts", "blk")),
        P("parts", None),
        P(("parts", "blk"), None),
        P(("parts", "blk"), None),
        P(("parts", "blk")),
    )
    out_specs = P(("parts", "blk"), "sub")
    return jax.shard_map(body, mesh=mesh, in_specs=in_specs, out_specs=out_specs, check_vma=False)
```
